512 devices in a mesh: dom: 128 (over y, z, core), feat: 4 (over x).
Axes of the slice: x: 4, y: 4, z: 16, core: 2. Of those that a mesh axis runs over, the one named last changes fastest.
Arguments:
- node_feats: bfloat16 [131072, 512], P('dom', 'feat'), may hold values from -6 to 6
- neigh_weight: bfloat16 [1024, 512], P(None, 'feat'), may hold values from -0.25 to 0.25
- bias: float32 [512], P('feat'), may hold values from -3 to 3
- out_grad: bfloat16 [131072, 512], P('dom', 'feat'), may hold values from -6 to 6
- tile_values: bfloat16 [11264, 128, 128], P('dom'), may hold values from 0 to 1, as said below
- tile_src: int32 [11264], P('dom'), may hold values from 0 to 43, as said below
- tile_dst: int32 [11264], P('dom'), may hold values from 0 to 7
- tile_count: int32 [128], P('dom'), may hold values from 22 to 88, as said below
- hub_rows: int32 [4096], P('dom'), may hold values from 0 to 1023
- send_rows: int32 [16384, 4], P('dom'), may hold values from 0 to 1023
Outputs:
- layer_out: bfloat16 [131072, 512], P('dom', 'feat')
- node_grad: bfloat16 [131072, 512], P('dom', 'feat')
- weight_grad: float32 [1024, 512], P(None, 'feat')
- bias_grad: float32 [512], P('feat')
The draws below stay inside these ranges and needn't reach their ends.
Inputs may be any that keep to these rules, and one draw needn't show every extreme that they name: `tile_src`: in each partition tile t < 8 has source and destination block t, and the next 4 tiles have the halo blocks as sources in order; later tiles have any source block. `tile_count`: some partition has all 88 tiles live in every draw. `tile_values`: entries are 0 or 1; slots past a partition's live count hold arbitrary 0/1 entries.
All inputs are finite; a program needn't handle non-finite values.
Results may differ from the reference program's by a relative error of at most 0.007.
Values may be sent and summed in bfloat16 or wider, within the bound.
A program may use at most 64 MiB of HBM per device.

```python
import math
import jax
import jax.numpy as jnp
from jax import lax

D = 512
NODE_DEV = 1024
TILE = 128
TILES = 88
HALO_DEV = 512
HUB_DEV = 32
HUBS = 4096
CUT = 4
NODES = 131072
N_DOM = 128


def tile_structure(key):
    keys = jax.random.split(key, 6)
    dst_blocks = NODE_DEV // TILE
    halo_blocks = HALO_DEV // TILE
    src_blocks = (NODE_DEV + HALO_DEV + HUBS) // TILE
    first_hub = dst_blocks + halo_blocks
    position = jnp.arange(TILES, dtype=jnp.int32)[None, :]
    random_src = jax.random.randint(keys[0], (N_DOM, TILES), 0, src_blocks)
    random_dst = jax.random.randint(keys[1], (N_DOM, TILES), 0, dst_blocks)
    src_table = jnp.where(position < first_hub, position, random_src).astype(jnp.int32)
    dst_table = jnp.where(position < dst_blocks, position, random_dst).astype(jnp.int32)
    lowest = TILES // 4
    extra = jnp.min(jax.random.randint(keys[2], (3, N_DOM), 0, TILES - lowest + 1), axis=0)
    busiest = jax.random.randint(keys[3], (), 0, N_DOM)
    counts = jnp.where(jnp.arange(N_DOM) == busiest, TILES, lowest + extra).astype(jnp.int32)
    keep = jax.random.randint(keys[4], (N_DOM, NODE_DEV), 0, 32) > 0
    row_index = (dst_table[:, :, None] * TILE + jnp.arange(TILE, dtype=jnp.int32)[None, None, :]).reshape(N_DOM, TILES * TILE)
    keep_rows = jnp.take_along_axis(keep, row_index, axis=1).reshape(N_DOM, TILES, TILE, 1)
    density = jnp.where(src_table >= first_hub, 2, jnp.where(src_table >= dst_blocks, 4, 1))[:, :, None, None]
    entries = jax.random.randint(keys[5], (N_DOM, TILES, TILE, TILE), 0, 32)
    values = jnp.where((entries < density) & keep_rows, 1.0, 0.0).astype(jnp.float32)
    return (src_table.reshape(N_DOM * TILES), dst_table.reshape(N_DOM * TILES), counts, values.reshape(N_DOM * TILES, TILE, TILE))


def draw_tile_values(key, part):
    shared = tile_structure(key)
    return shared[3].astype(jnp.bfloat16)


def draw_tile_src(key, part):
    shared = tile_structure(key)
    return shared[0]


def draw_tile_dst(key, part):
    shared = tile_structure(key)
    return shared[1]


def draw_tile_count(key, part):
    shared = tile_structure(key)
    return shared[2]


def touch_ends(array, key, low, high):
    spot = [jax.random.randint(jax.random.fold_in(key, axis), (), 0, length) for axis, length in enumerate(array.shape)]
    main_axis = array.shape.index(max(array.shape))
    beside = spot[:main_axis] + [(spot[main_axis] + 1) % array.shape[main_axis]] + spot[main_axis + 1:]
    return array.at[tuple(spot)].set(low).at[tuple(beside)].set(high)


def level_of(rng, extent, pieces, low, largest):
    def one(axis_at, shards_of):
        draws = jax.random.uniform(jax.random.fold_in(jax.random.fold_in(rng, 6), axis_at), (shards_of,), jnp.float32, low / len(pieces), largest / len(pieces))
        return jnp.repeat(jnp.exp(draws), extent[axis_at] // shards_of).reshape((-1,) + (1,) * (len(extent) - axis_at - 1))

    factor_of = one(*pieces[0])
    for cut in pieces[1:]:
        factor_of = factor_of * one(*cut)
    return factor_of


def centred(own_key, dims, width, limit, pieces=(), kind=jnp.bfloat16):
    gain = level_of(own_key, dims, pieces, -0.22, 0.18) if pieces else 1.0
    drawn = jax.random.normal(own_key, dims, jnp.float32) * width * gain
    return jnp.minimum(jnp.maximum(drawn, -limit), limit).astype(kind)


def setup_inputs(seed: int = 0) -> dict:
    key_list = jax.random.split(jax.random.key(seed), 11)
    node_feats = centred(key_list[0], (NODES, D), 1.0, 6.0, ((0, 128), (1, 4)))
    neigh_weight = centred(key_list[1], (2 * D, D), D ** -0.5, 0.25, ((1, 4),))
    bias = centred(key_list[2], (D,), 0.5, 3.0, ((0, 4),), jnp.float32)
    out_grad = centred(key_list[3], (NODES, D), 1.0, 6.0, ((0, 128), (1, 4)))
    tile_values = draw_tile_values(jax.random.fold_in(key_list[10], 71), 0)
    tile_src = draw_tile_src(jax.random.fold_in(key_list[10], 71), 0)
    tile_dst = draw_tile_dst(jax.random.fold_in(key_list[10], 71), 0)
    tile_count = draw_tile_count(jax.random.fold_in(key_list[10], 71), 0)
    hub_rows = touch_ends(jax.random.randint(key_list[8], (HUBS,), 0, NODE_DEV), jax.random.fold_in(key_list[8], 1), 0, NODE_DEV - 1).astype(jnp.int32)
    send_rows = touch_ends(jax.random.randint(key_list[9], (N_DOM * N_DOM, CUT), 0, NODE_DEV), jax.random.fold_in(key_list[9], 1), 0, NODE_DEV - 1).astype(jnp.int32)
    return dict(node_feats=node_feats, neigh_weight=neigh_weight, bias=bias, out_grad=out_grad, tile_values=tile_values, tile_src=tile_src, tile_dst=tile_dst, tile_count=tile_count, hub_rows=hub_rows, send_rows=send_rows)


HIGHEST_PREC = lax.Precision.HIGHEST

def silu_slope(pre_act):
    sigmoid_val = jax.nn.sigmoid(pre_act)
    return sigmoid_val * (1.0 + pre_act * (1.0 - sigmoid_val))

def tile_masks(live_count, src_tile, dst_tile, dst_blocks, src_blocks):
    live_tiles = (jnp.arange(TILES) < live_count).astype(jnp.float32)
    dst_hot = (dst_tile[:, None] == jnp.arange(dst_blocks)[None, :]).astype(jnp.float32) * live_tiles[:, None]
    src_hot = (src_tile[:, None] == jnp.arange(src_blocks)[None, :]).astype(jnp.float32) * live_tiles[:, None]
    return (dst_hot, src_hot)

def reference(node_feats, neigh_weight, bias, out_grad, tile_values, tile_src, tile_dst, tile_count, hub_rows, send_rows):
    dst_blocks = NODE_DEV // TILE
    src_blocks = (NODE_DEV + HALO_DEV + HUBS) // TILE
    owners = jnp.arange(HUBS, dtype=jnp.int32) // HUB_DEV
    hub_index = (owners * NODE_DEV + hub_rows).astype(jnp.int32)
    send_table = send_rows.reshape(N_DOM, N_DOM, CUT)
    senders = jnp.arange(N_DOM, dtype=jnp.int32)[:, None, None] * NODE_DEV
    halo_index = jnp.transpose(send_table + senders, (1, 0, 2)).reshape(N_DOM, HALO_DEV).astype(jnp.int32)
    hub_table = node_feats[hub_index]
    block_vals = tile_values.reshape(N_DOM, TILES, TILE, TILE)
    src_tiles = tile_src.reshape(N_DOM, TILES)
    dst_tiles = tile_dst.reshape(N_DOM, TILES)
    own_feats = node_feats.reshape(N_DOM, NODE_DEV, D)

    def aggregate(packed):
        values, src_tile, dst_tile, live_count, local_feats, halo_rows = packed
        dst_hot, src_hot = tile_masks(live_count, src_tile, dst_tile, dst_blocks, src_blocks)
        tiles_wide = values.astype(jnp.float32)
        degree = jnp.einsum('tn,ti->ni', dst_hot, lax.optimization_barrier(jnp.sum(tiles_wide, axis=2)), precision=HIGHEST_PREC).reshape(NODE_DEV)
        inverse = 1.0 / jnp.maximum(degree, 1.0)
        source_rows = jnp.concatenate([local_feats, node_feats[halo_rows], hub_table], axis=0)
        picked = source_rows.reshape(src_blocks, TILE, D)[src_tile].astype(jnp.float32)
        products = jnp.einsum('tij,tjf->tif', tiles_wide, picked, precision=HIGHEST_PREC)
        row_sums = jnp.einsum('tn,tif->nif', dst_hot, products, precision=HIGHEST_PREC).reshape(NODE_DEV, D)
        return ((row_sums * inverse[:, None]).astype(jnp.bfloat16), inverse)
    neigh_mean, inverse = lax.map(aggregate, (block_vals, src_tiles, dst_tiles, tile_count, own_feats, halo_index))
    neigh_mean = neigh_mean.reshape(NODES, D)
    inverse = inverse.reshape(NODES)
    joined = jnp.concatenate([node_feats, neigh_mean], axis=1)
    pre_act = jnp.dot(joined, neigh_weight, preferred_element_type=jnp.float32) + bias
    layer_out = jax.nn.silu(pre_act).astype(jnp.bfloat16)
    grad_pre = (out_grad.astype(jnp.float32) * silu_slope(pre_act)).astype(jnp.bfloat16)
    grad_scale = 1.0 / math.sqrt(NODES)
    weight_grad = jnp.dot(joined.T, grad_pre, preferred_element_type=jnp.float32) * grad_scale
    bias_grad = lax.optimization_barrier(jnp.sum(grad_pre.astype(jnp.float32), axis=0)) * grad_scale
    grad_cat = jnp.dot(grad_pre, neigh_weight.T, preferred_element_type=jnp.float32)
    grad_self = grad_cat[:, :D]
    grad_mean = (grad_cat[:, D:] * inverse[:, None]).astype(jnp.bfloat16).reshape(N_DOM, NODE_DEV, D)

    def spread_back(running, packed):
        values, src_tile, dst_tile, live_count, grad_block, halo_rows, device = packed
        dst_hot, src_hot = tile_masks(live_count, src_tile, dst_tile, dst_blocks, src_blocks)
        tiles_wide = values.astype(jnp.float32)
        chosen = grad_block.reshape(dst_blocks, TILE, D)[dst_tile].astype(jnp.float32)
        back_terms = jnp.einsum('tij,tif->tjf', tiles_wide, chosen, precision=HIGHEST_PREC)
        spread = jnp.einsum('ts,tjf->sjf', src_hot, back_terms, precision=HIGHEST_PREC).reshape(src_blocks * TILE, D)
        halo_part = lax.optimization_barrier(spread[NODE_DEV:NODE_DEV + HALO_DEV].astype(jnp.bfloat16)).astype(jnp.float32)
        spread = jnp.concatenate([spread[:NODE_DEV], halo_part, spread[NODE_DEV + HALO_DEV:]], axis=0)
        local_index = device * NODE_DEV + jnp.arange(NODE_DEV, dtype=jnp.int32)
        all_index = jnp.concatenate([local_index, halo_rows, hub_index]).astype(jnp.int32)
        return (running.at[all_index].add(spread), None)
    devices = jnp.arange(N_DOM, dtype=jnp.int32)
    running, _ = lax.scan(spread_back, grad_self, (block_vals, src_tiles, dst_tiles, tile_count, grad_mean, halo_index, devices))
    node_grad = running.astype(jnp.bfloat16)
    return (layer_out, node_grad, weight_grad, bias_grad)
```

```python
import functools
import math

import jax
import jax.numpy as jnp
from jax import lax
from jax.experimental import pallas as pl
from jax.experimental.pallas import tpu as pltpu
from jax.sharding import PartitionSpec as P

BF16 = jnp.bfloat16
F32 = jnp.float32
CORES = 2
Y_CHIPS = 4


def dot(a, b):
    return jnp.dot(a, b, preferred_element_type=F32)


def dot_nt(a, b):
    return lax.dot_general(a, b, (((1,), (1,)), ((), ())), preferred_element_type=F32)


def dot_tn(a, b):
    return lax.dot_general(a, b, (((0,), (0,)), ((), ())), preferred_element_type=F32)


class Group:
    def __init__(self, size, me, device):
        self.size, self.me, self.device = size, me, device

    def each(self, body):
        if self.size <= 4:
            for step in range(1, self.size):
                body(step, lax.rem(self.me + step, self.size))
        else:

            def loop(step, carry):
                body(step, lax.rem(self.me + step, self.size))
                return carry

            lax.fori_loop(1, self.size, loop, 0)


class Exchange:
    def __init__(self, group, src, dst, sems):
        self.group, self.src, self.dst, self.sems = group, src, dst, sems

    def copy(self, step, peer, landing):
        return pltpu.make_async_remote_copy(
            src_ref=self.src(peer),
            dst_ref=self.dst(landing),
            send_sem=self.sems.at[0, step],
            recv_sem=self.sems.at[1, landing],
            device_id=self.group.device(peer),
            device_id_type=pl.DeviceIdType.MESH,
        )

    def start_one(self, step, peer):
        self.copy(step, peer, self.group.me).start()

    def start(self):
        self.group.each(self.start_one)

    def wait_one(self, step, peer):
        self.copy(step, peer, peer).wait_recv()

    def wait(self):
        self.group.each(self.wait_one)

    def drain(self):
        self.group.each(lambda step, peer: self.copy(step, peer, self.group.me).wait_send())


def kernel(
    dims,
    nf,
    weight,
    bias,
    out_grad,
    tiles,
    idx_col,
    idx_row,
    prev,
    last,
    layer_out,
    node_grad,
    weight_grad,
    bias_grad,
    tile_buf,
    acc_tiles,
    acc_tiles_t,
    adj,
    adj_t,
    out_halo,
    st1,
    st2,
    halo_z,
    halo,
    hub,
    deg,
    acc,
    selfc,
    meanc,
    ogc,
    wfull,
    biasc,
    mean,
    pre,
    lo_send,
    lo_recv,
    gp,
    gm_send,
    gm,
    gs_send,
    gs_recv,
    wg32,
    wgb,
    wg_core,
    wx_send,
    wx_recv,
    wx_own,
    wy_send,
    wy_recv,
    wy_own,
    wz_send,
    wz_recv,
    wout,
    bias_core,
    hs32,
    hsb,
    hs_core,
    hy_send,
    hy_recv,
    hy_own,
    hz_send,
    hz_recv,
    halo_b,
    halo_zb,
    rt1,
    halo_m,
    rt2,
    total,
    tile_sem,
    s_yc,
    s_z,
    s_hz,
    s_hy,
    s_hc,
    s_xs,
    s_xo,
    s_xw,
    s_xb,
    s_wc,
    s_xm,
    s_xl,
    s_xg,
    s_xgs,
    s_gc,
    s_gx,
    s_gy,
    s_gz,
    s_az,
    s_ay,
    s_ac,
    s_bc,
    s_bhc,
    s_bhy,
    s_bhz,
    s_rz,
    s_ryc,
):
    Y, Z, C, X, N, T, NT, F, HD, CUT, scale = dims
    D = X * F
    R = N // X
    HALO = Y * Z * C * CUT
    NB = N // T
    SB = (N + HALO + Y * Z * C * HD) // T
    dom, x = lax.axis_index("dom"), lax.axis_index("feat")
    c = lax.rem(dom, C)
    z = lax.rem(lax.div(dom, C), Z)
    y = lax.div(dom, C * Z)
    yc = y * C + c

    def at(yy, zz, cc):
        return ((yy * Z + zz) * C + cc, x)

    gyc = Group(Y * C, yc, lambda p: at(lax.div(p, C), z, lax.rem(p, C)))
    gz = Group(Z, z, lambda p: at(y, p, c))
    gy = Group(Y, y, lambda p: at(p, z, c))
    gc = Group(C, c, lambda p: at(y, z, p))
    gx = Group(X, x, lambda p: (dom, p))

    fetch = pltpu.make_async_copy(tiles, tile_buf, tile_sem)
    fetch.start()

    barrier = pltpu.get_barrier_semaphore()
    for group in (gyc, gz, gx):
        group.each(
            lambda step, peer, group=group: pl.semaphore_signal(
                barrier, inc=1, device_id=group.device(peer), device_id_type=pl.DeviceIdType.MESH
            )
        )

    def pick(i, carry):
        rows = pl.ds(pl.multiple_of(i * T, T), T)
        hot = (idx_col[rows, :] == lax.broadcasted_iota(jnp.int32, (T, N), 1)).astype(BF16)
        out_halo[rows, :] = dot(hot, nf[...]).astype(BF16)
        return carry

    lax.fori_loop(0, HALO // T, pick, 0)
    hub_hot = (
        idx_col[pl.ds(HALO, HD), :] == lax.broadcasted_iota(jnp.int32, (HD, N), 1)
    ).astype(BF16)
    hub[y, z, c] = dot(hub_hot, nf[...]).astype(BF16)
    pl.semaphore_wait(barrier, Y * C + Z + X - 3)

    def rows_of(p):
        return pl.ds(pl.multiple_of(p * R, R), R)

    def cols_of(p):
        return pl.ds(pl.multiple_of(p * F, F), F)

    ZC = Z * CUT
    YCC = Y * C * CUT
    ex_yc = Exchange(
        gyc,
        lambda p: out_halo.at[pl.ds(pl.multiple_of(p * ZC, ZC), ZC)],
        lambda p: st1.at[p],
        s_yc,
    )
    ex_hz = Exchange(gz, lambda p: hub.at[y, z, c], lambda p: hub.at[y, p, c], s_hz)
    ex_yc.start()
    ex_hz.start()
    st1[yc] = out_halo[pl.ds(pl.multiple_of(yc * ZC, ZC), ZC), :]

    half = D
    wrows = pl.ds(pl.multiple_of(c * half, half), half)
    ex_xs = Exchange(
        gx, lambda p: nf.at[rows_of(p)], lambda p: selfc.at[:, cols_of(p)], s_xs
    )
    ex_xw = Exchange(
        gx, lambda p: weight.at[wrows], lambda p: wfull.at[wrows, cols_of(p)], s_xw
    )
    ex_xo = Exchange(
        gx, lambda p: out_grad.at[rows_of(p)], lambda p: ogc.at[:, cols_of(p)], s_xo
    )
    ex_xb = Exchange(gx, lambda p: bias, lambda p: biasc.at[:, cols_of(p)], s_xb)
    ex_xs.start()
    ex_xw.start()
    ex_xb.start()
    ex_xo.start()
    selfc[:, cols_of(x)] = nf[rows_of(x), :]
    ogc[:, cols_of(x)] = out_grad[rows_of(x), :]
    wfull[:, cols_of(x)] = weight[...]
    biasc[:, cols_of(x)] = bias[...]

    fetch.wait()
    acc_tiles[NT] = jnp.zeros((T, T), BF16)
    acc_tiles_t[NT] = jnp.zeros((T, T), BF16)

    def add_tile(t, carry):
        value = tile_buf[t].astype(F32) + acc_tiles[prev[t]].astype(F32)
        acc_tiles[t] = value.astype(BF16)
        acc_tiles_t[t] = value.T.astype(BF16)
        return carry

    lax.fori_loop(0, NT, add_tile, 0)

    def perm(rows, source_of):
        r = lax.broadcasted_iota(jnp.int32, (rows, rows), 0)
        i = lax.broadcasted_iota(jnp.int32, (rows, rows), 1)
        return (source_of(r) == i).astype(BF16)

    def log2(n):
        return n.bit_length() - 1

    def div_(a, n):
        return lax.shift_right_logical(a, log2(n))

    def mod_(a, n):
        return a & (n - 1)

    def z_major(r):
        return (mod_(div_(r, CUT), Y * C) * Z + div_(r, YCC)) * CUT + mod_(r, CUT)

    def yc_major(r):
        return (mod_(div_(r, CUT), Z) * (Y * C) + div_(r, ZC)) * CUT + mod_(r, CUT)

    def to_dom(r):
        yy = div_(r, Z * C * CUT)
        zz = mod_(div_(r, C * CUT), Z)
        return (zz * Y + yy) * (C * CUT) + mod_(r, C * CUT)

    def from_dom(r):
        zz = div_(r, Y * C * CUT)
        yy = mod_(div_(r, C * CUT), Y)
        return (yy * Z + zz) * (C * CUT) + mod_(r, C * CUT)

    ex_yc.wait()
    halo_z[...] = (
        dot(perm(HALO, z_major), st1[...].reshape(HALO, F)).astype(BF16).reshape(Z, YCC, F)
    )
    ex_z = Exchange(gz, lambda p: halo_z.at[p], lambda p: st2.at[p], s_z)
    ex_z.start()
    st2[z] = halo_z[z]

    ex_hz.wait()
    ex_hy = Exchange(gy, lambda p: hub.at[y, :, c], lambda p: hub.at[p, :, c], s_hy)
    ex_hy.start()

    def hub_to_core(yy):
        return pltpu.make_async_remote_copy(
            src_ref=hub.at[yy, :, c],
            dst_ref=hub.at[yy, :, c],
            send_sem=s_hc.at[0, yy],
            recv_sem=s_hc.at[1, yy],
            device_id=gc.device(1 - c),
            device_id_type=pl.DeviceIdType.MESH,
        )

    def hub_from_core(yy):
        return pltpu.make_async_remote_copy(
            src_ref=hub.at[yy, :, 1 - c],
            dst_ref=hub.at[yy, :, 1 - c],
            send_sem=s_hc.at[0, yy],
            recv_sem=s_hc.at[1, yy],
            device_id=gc.device(1 - c),
            device_id_type=pl.DeviceIdType.MESH,
        )

    hub_to_core(y).start()

    def place(k, carry):
        for h in range(2):
            for n in range(NB):
                slot = last[n * SB + 2 * k + h]
                adj[k, n * T : (n + 1) * T, h * T : (h + 1) * T] = acc_tiles[slot]
                adj_t[k, h * T : (h + 1) * T, n * T : (n + 1) * T] = acc_tiles_t[slot]
        return carry

    lax.fori_loop(0, SB // 2, place, 0)

    gy.each(lambda step, peer: (ex_hy.wait_one(step, peer), hub_to_core(peer).start())[0])

    ones = jnp.ones((2 * T, F), BF16)
    deg[...] = jnp.zeros_like(deg)
    acc[...] = jnp.zeros_like(acc)

    def add_deg(k, carry):
        deg[...] += dot(adj[k], ones)
        return carry

    lax.fori_loop(0, SB // 2, add_deg, 0)
    deg[...] = 1.0 / jnp.maximum(deg[...], 1.0)
    inv_rows = deg[rows_of(x), :]

    def add_own(k, carry):
        acc[...] += dot(adj[k], nf[pl.ds(pl.multiple_of(k * 2 * T, 2 * T), 2 * T), :])
        return carry

    own_k = NB // 2
    lax.fori_loop(0, own_k, add_own, 0)

    ex_z.wait()
    halo[...] = dot(perm(HALO, to_dom), st2[...].reshape(HALO, F)).astype(BF16)
    halo_k = HALO // (2 * T)

    def add_halo(k, carry):
        acc[...] += dot(adj[own_k + k], halo[pl.ds(pl.multiple_of(k * 2 * T, 2 * T), 2 * T), :])
        return carry

    lax.fori_loop(0, halo_k, add_halo, 0)
    hub_first = own_k + halo_k
    zstep = 2 * T // (C * HD)
    per_y = Z // zstep

    def add_hub(k, carry):
        rows = hub[lax.div(k, per_y), pl.ds(lax.rem(k, per_y) * zstep, zstep)]
        acc[...] += dot(adj[hub_first + k], rows.reshape(2 * T, F))
        return carry

    hub_from_core(y).wait_recv()
    gy.each(lambda step, peer: hub_from_core(peer).wait_recv())
    lax.fori_loop(0, Y * per_y, add_hub, 0)
    mean[...] = (acc[...] * deg[...]).astype(BF16)

    ex_xm = Exchange(
        gx, lambda p: mean.at[rows_of(p)], lambda p: meanc.at[:, cols_of(p)], s_xm
    )
    ex_xm.start()
    meanc[:, cols_of(x)] = mean[rows_of(x), :]

    def w_core(p, cc, step):
        part = wfull.at[pl.ds(pl.multiple_of(cc * half, half), half), cols_of(p)]
        return pltpu.make_async_remote_copy(
            src_ref=part,
            dst_ref=part,
            send_sem=s_wc.at[0, p],
            recv_sem=s_wc.at[1, p],
            device_id=gc.device(1 - c),
            device_id_type=pl.DeviceIdType.MESH,
        )

    gx.each(
        lambda step, peer: (ex_xw.wait_one(step, peer), w_core(peer, c, step).start())[0]
    )
    ex_xs.wait()
    ex_xb.wait()
    ex_xo.wait()
    gx.each(lambda step, peer: w_core(peer, 1 - c, step).wait_recv())
    pre[...] = dot(selfc[...], wfull[0:D, :]) + biasc[0:1, :]
    ex_xm.wait()
    pre_act = pre[...] + dot(meanc[...], wfull[D : 2 * D, :])
    sig = jax.nn.sigmoid(pre_act)
    lo_send[...] = (pre_act * sig).astype(BF16)
    gp[...] = (ogc[...].astype(F32) * (sig * (1.0 + pre_act * (1.0 - sig)))).astype(BF16)
    cat_mean = dot_nt(gp[...], wfull[D : 2 * D, :])
    for j in range(X):
        gm_send[j] = (cat_mean[:, j * F : (j + 1) * F] * inv_rows).astype(BF16)
    ex_xg = Exchange(gx, lambda p: gm_send.at[p], lambda p: gm.at[p], s_xg)
    ex_xg.start()
    gm[x] = gm_send[x]

    for q in range(2 * D // T):
        src = selfc if q * T < D else meanc
        col = (q * T) % D
        part = dot_tn(src[:, col : col + T], gp[...])
        row = (q * T) % D
        wg32[q * T // D, row : row + T, :] = part
        wgb[q * T // D, row : row + T, :] = part.astype(BF16)
    ex_gc = Exchange(gc, lambda p: wgb.at[p], lambda p: wg_core.at[p], s_gc)
    ex_gc.start()
    ex_xl = Exchange(
        gx, lambda p: lo_send.at[:, cols_of(p)], lambda p: lo_recv.at[p], s_xl
    )
    ex_xl.start()
    lo_recv[x] = lo_send[:, cols_of(x)]
    bias_sum = jnp.sum(gp[...].astype(F32), axis=0, keepdims=True)

    def bias_rows(value):
        full = jnp.broadcast_to(value, (8, F))
        high = full.astype(BF16)
        low = (full - high.astype(F32)).astype(BF16)
        return jnp.concatenate([high.astype(F32), low.astype(F32)], axis=0).astype(BF16)

    def bias_of(rows):
        wide = rows.astype(F32)
        return wide[0:8] + wide[8:16]

    cat_self = dot_nt(gp[...], wfull[0:D, :])
    for j in range(X):
        gs_send[j] = cat_self[:, j * F : (j + 1) * F].astype(BF16)
    ex_xgs = Exchange(gx, lambda p: gs_send.at[p], lambda p: gs_recv.at[p], s_xgs)
    ex_xgs.start()
    gs_recv[x] = gs_send[x]

    ex_xg.wait()
    def spread(k):
        return dot(adj_t[k], gm[...].reshape(N, F))

    class Core:
        def __init__(self, yy):
            self.yy = yy

        def copy(self):
            return pltpu.make_async_remote_copy(
                src_ref=hsb.at[1 - c, self.yy],
                dst_ref=hs_core.at[self.yy],
                send_sem=s_bhc.at[0, self.yy],
                recv_sem=s_bhc.at[1, self.yy],
                device_id=gc.device(1 - c),
                device_id_type=pl.DeviceIdType.MESH,
            )

    for yy in range(Y):

        def back_hub(k, carry, yy=yy):
            rows = spread(hub_first + yy * per_y + k).reshape(zstep, C, HD, F)
            for cc in range(C):
                hs32[cc, yy, pl.ds(k * zstep, zstep)] = rows[:, cc]
                hsb[cc, yy, pl.ds(k * zstep, zstep)] = rows[:, cc].astype(BF16)
            return carry

        lax.fori_loop(0, per_y, back_hub, 0)
        Core(yy).copy().start()

    def back_halo(k, carry):
        halo_b[pl.ds(pl.multiple_of(k * 2 * T, 2 * T), 2 * T), :] = spread(own_k + k).astype(BF16)
        return carry

    lax.fori_loop(0, halo_k, back_halo, 0)
    halo_zb[...] = dot(perm(HALO, from_dom), halo_b[...]).astype(BF16).reshape(Z, YCC, F)
    ex_rz = Exchange(gz, lambda p: halo_zb.at[p], lambda p: rt1.at[p], s_rz)
    ex_rz.start()
    rt1[z] = halo_zb[z]

    ex_bhy = Exchange(gy, lambda p: hy_send.at[p], lambda p: hy_recv.at[p], s_bhy)
    for yy in range(Y):
        Core(yy).copy().wait_recv()
        pair = hs32[c, yy] + hs_core[yy].astype(F32)
        hy_own[yy] = pair
        hy_send[yy] = pair.astype(BF16)
    ex_bhy.start()

    ex_gc.wait()
    for j in range(X):
        block = wg32[c, :, j * F : (j + 1) * F] + wg_core[1 - c, :, j * F : (j + 1) * F].astype(F32)
        wx_own[j, 0:D, :] = block
        wx_send[j, 0:D, :] = block.astype(BF16)
        bias_j = bias_sum[:, j * F : (j + 1) * F]
        wx_own[j, D : D + 8, :] = jnp.broadcast_to(bias_j, (8, F))
        wx_send[j, D : D + 16, :] = bias_rows(bias_j)
    ex_gx = Exchange(gx, lambda p: wx_send.at[p], lambda p: wx_recv.at[p], s_gx)
    ex_gx.start()

    def back_own(k, carry):
        rows = pl.ds(pl.multiple_of(k * 2 * T, 2 * T), 2 * T)
        total[rows, :] = spread(k)
        return carry

    lax.fori_loop(0, own_k, back_own, 0)

    ex_rz.wait()
    halo_m[...] = (
        dot(perm(HALO, yc_major), rt1[...].reshape(HALO, F)).astype(BF16).reshape(Y * C, ZC, F)
    )
    ex_ryc = Exchange(gyc, lambda p: halo_m.at[p], lambda p: rt2.at[p], s_ryc)
    ex_ryc.start()
    rt2[yc] = halo_m[yc]

    ex_bhy.wait()
    hy_recv[y] = jnp.zeros((Z, HD, F), BF16)
    hub_y = hy_own[y]
    for yy in range(Y):
        hub_y = hub_y + hy_recv[yy].astype(F32)
    hy_own[y] = hub_y
    hz_send[...] = hub_y.astype(BF16)
    ex_bhz = Exchange(gz, lambda p: hz_send.at[p], lambda p: hz_recv.at[p], s_bhz)
    ex_bhz.start()

    ex_gx.wait()
    wx_recv[x] = jnp.zeros((D + 16, F), BF16)
    wsum = wx_own[x, 0:D, :]
    bsum = wx_own[x, D : D + 8, :]
    for j in range(X):
        wsum = wsum + wx_recv[j, 0:D, :].astype(F32)
        bsum = bsum + bias_of(wx_recv[j, D : D + 16, :])
    DY = D // Y
    for j in range(Y):
        block = wsum[j * DY : (j + 1) * DY]
        wy_own[j] = block
        wy_send[j, 0:DY, :] = block.astype(BF16)
        wy_send[j, DY : DY + 16, :] = bias_rows(bsum[0:1])
    ex_gy = Exchange(gy, lambda p: wy_send.at[p], lambda p: wy_recv.at[p], s_gy)
    ex_gy.start()

    ex_xl.wait()
    for j in range(X):
        layer_out[j * R : (j + 1) * R, :] = lo_recv[j]
    ex_xgs.wait()
    for j in range(X):
        total[j * R : (j + 1) * R, :] += gs_recv[j].astype(F32)

    ex_gy.wait()
    wy_recv[y] = jnp.zeros((DY + 16, F), BF16)
    wsum = wy_own[y]
    for j in range(Y):
        wsum = wsum + wy_recv[j, 0:DY, :].astype(F32)
        bsum = bsum + bias_of(wy_recv[j, DY : DY + 16, :])
    DZ = DY // Z
    for j in range(Z):
        wz_send[j, 0:DZ, :] = wsum[j * DZ : (j + 1) * DZ]
        wz_send[j, DZ : DZ + 8, :] = bsum
    ex_gz = Exchange(gz, lambda p: wz_send.at[p], lambda p: wz_recv.at[p], s_gz)
    ex_gz.start()

    ex_ryc.wait()
    ex_bhz.wait()
    hz_recv[z] = jnp.zeros((HD, F), BF16)
    hub_mine = hy_own[y, z] + jnp.sum(hz_recv[...].astype(F32), axis=0)
    high = hub_mine.astype(BF16)
    low = (hub_mine - high.astype(F32)).astype(BF16)

    ex_gz.wait()
    wz_recv[z] = wz_send[z]
    zsum = jnp.sum(wz_recv[...], axis=0) * scale
    wout[c, y, z] = zsum[0:DZ]
    bias_core[c] = zsum[DZ : DZ + 8]
    ex_az = Exchange(gz, lambda p: wout.at[c, y, z], lambda p: wout.at[c, y, p], s_az)
    ex_az.start()
    ex_bc = Exchange(gc, lambda p: bias_core.at[c], lambda p: bias_core.at[p], s_bc)
    ex_bc.start()

    hot_all = idx_row[...]
    returned = jnp.concatenate([rt2[...].reshape(HALO, F), high, low], axis=0)
    for n in range(NB):
        hot = (
            lax.broadcasted_iota(jnp.int32, (T, HALO + 2 * HD), 0) + n * T == hot_all
        ).astype(BF16)
        rows = total[n * T : (n + 1) * T, :] + dot(hot, returned)
        node_grad[n * T : (n + 1) * T, :] = rows.astype(BF16)

    ex_az.wait()
    ex_ay = Exchange(gy, lambda p: wout.at[c, y], lambda p: wout.at[c, p], s_ay)
    ex_ay.start()
    ex_ay.wait()
    ex_ac = Exchange(gc, lambda p: wout.at[c], lambda p: wout.at[p], s_ac)
    ex_ac.start()
    ex_bc.wait()
    bias_grad[...] = bias_core[0] + bias_core[1]
    ex_ac.wait()
    weight_grad[...] = wout[...].reshape(2 * D, F)

    for ex in (
        ex_yc, ex_z, ex_hz, ex_hy, ex_xs, ex_xw, ex_xo, ex_xb, ex_xm, ex_xl, ex_xg, ex_xgs,
        ex_gc, ex_gx, ex_gy, ex_gz, ex_az, ex_ay, ex_ac, ex_bc, ex_bhy, ex_bhz, ex_rz, ex_ryc,
    ):
        ex.drain()
    for yy in range(Y):
        Core(yy).copy().wait_send()
        hub_to_core(yy).wait_send()
    gx.each(lambda step, peer: w_core(peer, c, step).wait_send())


def per_device(
    sizes,
    node_feats,
    neigh_weight,
    bias,
    out_grad,
    tile_values,
    tile_src,
    tile_dst,
    tile_count,
    hub_rows,
    send_rows,
):
    Y, Z, C, X = sizes
    N, F = node_feats.shape
    NT, T = tile_values.shape[:2]
    CUT = send_rows.shape[1]
    HD = hub_rows.shape[0]
    DOM = Y * Z * C
    HALO = DOM * CUT
    NB, SB = N // T, (N + HALO + DOM * HD) // T
    D, R = X * F, N // X
    K = SB // 2
    ZC, YCC = Z * CUT, Y * C * CUT
    DY = D // Y
    DZ = DY // Z

    at = jnp.arange(NT, dtype=jnp.int32)
    key = jnp.where(at < tile_count[0], tile_dst * SB + tile_src, -1)
    same = (key[:, None] == key[None, :]) & (at[None, :] < at[:, None])
    prev = jnp.max(jnp.where(same, at[None, :], -1), axis=1)
    prev = jnp.where(prev < 0, NT, prev)
    place = jnp.arange(NB * SB, dtype=jnp.int32)
    last = jnp.max(jnp.where(place[:, None] == key[None, :], at[None, :], -1), axis=1)
    last = jnp.where(last < 0, NT, last)
    sends = send_rows.reshape(Y, Z, C, CUT).transpose(0, 2, 1, 3).reshape(HALO)
    idx_col = jnp.concatenate([sends, hub_rows])[:, None]
    idx_row = jnp.concatenate([sends, hub_rows, hub_rows])[None, :]
    bias8 = jnp.broadcast_to(bias[None, :], (8, F))

    dims = (Y, Z, C, X, N, T, NT, F, HD, CUT, 1.0 / math.sqrt(N * DOM))
    vm = pl.BlockSpec(memory_space=pltpu.VMEM)
    sm = pl.BlockSpec(memory_space=pltpu.SMEM)
    anyspace = pl.BlockSpec(memory_space=pl.ANY)

    def b(*shape):
        return pltpu.VMEM(shape, BF16)

    def f(*shape):
        return pltpu.VMEM(shape, F32)

    def sem(n):
        return pltpu.SemaphoreType.DMA((2, n))

    scratch = dict(
        tile_buf=b(NT, T, T),
        acc_tiles=b(NT + 1, T, T),
        acc_tiles_t=b(NT + 1, T, T),
        adj=b(K, N, 2 * T),
        adj_t=b(K, 2 * T, N),
        out_halo=b(HALO, F),
        st1=b(Y * C, ZC, F),
        st2=b(Z, YCC, F),
        halo_z=b(Z, YCC, F),
        halo=b(HALO, F),
        hub=b(Y, Z, C, HD, F),
        deg=f(N, F),
        acc=f(N, F),
        selfc=b(R, D),
        meanc=b(R, D),
        ogc=b(R, D),
        wfull=b(2 * D, D),
        biasc=f(8, D),
        mean=b(N, F),
        pre=f(R, D),
        lo_send=b(R, D),
        lo_recv=b(X, R, F),
        gp=b(R, D),
        gm_send=b(X, R, F),
        gm=b(X, R, F),
        gs_send=b(X, R, F),
        gs_recv=b(X, R, F),
        wg32=f(C, D, D),
        wgb=b(C, D, D),
        wg_core=b(C, D, D),
        wx_send=b(X, D + 16, F),
        wx_recv=b(X, D + 16, F),
        wx_own=f(X, D + 8, F),
        wy_send=b(Y, DY + 16, F),
        wy_recv=b(Y, DY + 16, F),
        wy_own=f(Y, DY, F),
        wz_send=f(Z, DZ + 8, F),
        wz_recv=f(Z, DZ + 8, F),
        wout=f(C, Y, Z, DZ, F),
        bias_core=f(C, 8, F),
        hs32=f(C, Y, Z, HD, F),
        hsb=b(C, Y, Z, HD, F),
        hs_core=b(Y, Z, HD, F),
        hy_send=b(Y, Z, HD, F),
        hy_recv=b(Y, Z, HD, F),
        hy_own=f(Y, Z, HD, F),
        hz_send=b(Z, HD, F),
        hz_recv=b(Z, HD, F),
        halo_b=b(HALO, F),
        halo_zb=b(Z, YCC, F),
        rt1=b(Z, YCC, F),
        halo_m=b(Y * C, ZC, F),
        rt2=b(Y * C, ZC, F),
        total=f(N, F),
        tile_sem=pltpu.SemaphoreType.DMA,
        s_yc=sem(Y * C),
        s_z=sem(Z),
        s_hz=sem(Z),
        s_hy=sem(Y),
        s_hc=sem(Y),
        s_xs=sem(X),
        s_xo=sem(X),
        s_xw=sem(X),
        s_xb=sem(X),
        s_wc=sem(X),
        s_xm=sem(X),
        s_xl=sem(X),
        s_xg=sem(X),
        s_xgs=sem(X),
        s_gc=sem(C),
        s_gx=sem(X),
        s_gy=sem(Y),
        s_gz=sem(Z),
        s_az=sem(Z),
        s_ay=sem(Y),
        s_ac=sem(C),
        s_bc=sem(C),
        s_bhc=sem(Y),
        s_bhy=sem(Y),
        s_bhz=sem(Z),
        s_rz=sem(Z),
        s_ryc=sem(Y * C),
    )
    layer_out, node_grad, weight_grad, bias_grad = pl.pallas_call(
        functools.partial(kernel, dims),
        out_shape=(
            jax.ShapeDtypeStruct((N, F), BF16),
            jax.ShapeDtypeStruct((N, F), BF16),
            jax.ShapeDtypeStruct((2 * D, F), F32),
            jax.ShapeDtypeStruct((8, F), F32),
        ),
        in_specs=[vm, vm, vm, vm, anyspace, vm, vm, sm, sm],
        out_specs=(vm, vm, vm, vm),
        scratch_shapes=list(scratch.values()),
        compiler_params=pltpu.CompilerParams(
            collective_id=0, has_side_effects=True, vmem_limit_bytes=60 * 1024 * 1024
        ),
    )(node_feats, neigh_weight, bias8, out_grad, tile_values, idx_col, idx_row, prev, last)
    return layer_out, node_grad, weight_grad, bias_grad[0]


def solution(mesh, y_chips=Y_CHIPS):
    dom, feat = mesh.shape["dom"], mesh.shape["feat"]
    sizes = (y_chips, dom // (CORES * y_chips), CORES, feat)
    in_specs = (
        P("dom", "feat"),
        P(None, "feat"),
        P("feat"),
        P("dom", "feat"),
        P("dom", None, None),
        P("dom"),
        P("dom"),
        P("dom"),
        P("dom"),
        P("dom", None),
    )
    out_specs = (P("dom", "feat"), P("dom", "feat"), P(None, "feat"), P("feat"))
    return jax.shard_map(
        functools.partial(per_device, sizes),
        mesh=mesh,
        in_specs=in_specs,
        out_specs=out_specs,
        check_vma=False,
    )
```

```python
import functools
import math
import types

import jax
import jax.numpy as jnp
from jax import lax
from jax.experimental import pallas as pl
from jax.experimental.pallas import tpu as pltpu
from jax.sharding import PartitionSpec as P

BF16 = jnp.bfloat16
F32 = jnp.float32
CORES = 2
Y_CHIPS = 4


def dot(a, b):
    return jnp.dot(a, b, preferred_element_type=F32)


def dot_nt(a, b):
    return lax.dot_general(a, b, (((1,), (1,)), ((), ())), preferred_element_type=F32)


def dot_tn(a, b):
    return lax.dot_general(a, b, (((0,), (0,)), ((), ())), preferred_element_type=F32)


class Group:
    def __init__(self, size, me, device):
        self.size, self.me, self.device = size, me, device

    def each(self, body):
        if self.size <= 4:
            for step in range(1, self.size):
                body(step, lax.rem(self.me + step, self.size))
        else:

            def loop(step, carry):
                body(step, lax.rem(self.me + step, self.size))
                return carry

            lax.fori_loop(1, self.size, loop, 0)


class Exchange:
    def __init__(self, group, src, dst, sems):
        self.group, self.src, self.dst, self.sems = group, src, dst, sems

    def copy(self, step, peer, landing):
        return pltpu.make_async_remote_copy(
            src_ref=self.src(peer),
            dst_ref=self.dst(landing),
            send_sem=self.sems.at[0, step],
            recv_sem=self.sems.at[1, landing],
            device_id=self.group.device(peer),
            device_id_type=pl.DeviceIdType.MESH,
        )

    def start_to(self, peer):
        step = lax.rem(peer - self.group.me + self.group.size, self.group.size)
        self.copy(step, peer, self.group.me).start()

    def start_one(self, step, peer):
        self.copy(step, peer, self.group.me).start()

    def start(self):
        self.group.each(self.start_one)

    def wait_one(self, step, peer):
        self.copy(step, peer, peer).wait_recv()

    def wait(self):
        self.group.each(self.wait_one)

    def wait_then(self, after):
        def body(step, peer):
            self.wait_one(step, peer)
            after(peer)

        self.group.each(body)

    def drain(self):
        self.group.each(lambda step, peer: self.copy(step, peer, self.group.me).wait_send())


class Relay:
    def __init__(self, device, sems, src, dst):
        self.device, self.sems, self.src, self.dst = device, sems, src, dst

    def copy(self, slot):
        return pltpu.make_async_remote_copy(
            src_ref=self.src(slot),
            dst_ref=self.dst(slot),
            send_sem=self.sems.at[0, slot],
            recv_sem=self.sems.at[1, slot],
            device_id=self.device,
            device_id_type=pl.DeviceIdType.MESH,
        )

    def start(self, slot):
        self.copy(slot).start()


def log2(n):
    return n.bit_length() - 1


def div_(a, n):
    return lax.shift_right_logical(a, log2(n))


def mod_(a, n):
    return a & (n - 1)


def aligned(start, size):
    return pl.ds(pl.multiple_of(start, size), size)


def kernel(dims, names, *refs):
    r = types.SimpleNamespace(**dict(zip(names, refs)))
    Y, Z, C, X, N, T, NT, F, HD, CUT, scale = dims
    D = X * F
    R = N // X
    DOM = Y * Z * C
    HALO = DOM * CUT
    NB = N // T
    SB = (N + HALO + DOM * HD) // T
    ZC, YCC = Z * CUT, Y * C * CUT
    PERY = Z * C * HD
    DY = D // Y
    DZ = DY // Z
    dom, x = lax.axis_index("dom"), lax.axis_index("feat")
    c = lax.rem(dom, C)
    z = lax.rem(lax.div(dom, C), Z)
    y = lax.div(dom, C * Z)
    yc = y * C + c

    def at(yy, zz, cc):
        return ((yy * Z + zz) * C + cc, x)

    gyc = Group(Y * C, yc, lambda p: at(lax.div(p, C), z, lax.rem(p, C)))
    gz = Group(Z, z, lambda p: at(y, p, c))
    gy = Group(Y, y, lambda p: at(p, z, c))
    gc = Group(C, c, lambda p: at(y, z, p))
    gx = Group(X, x, lambda p: (dom, p))
    other_core = at(y, z, 1 - c)

    barrier = pltpu.get_barrier_semaphore()
    for group in (gyc, gz, gx):
        group.each(
            lambda step, peer, group=group: pl.semaphore_signal(
                barrier, inc=1, device_id=group.device(peer), device_id_type=pl.DeviceIdType.MESH
            )
        )

    def rows_of(p):
        return aligned(p * R, R)

    def cols_of(p):
        return aligned(p * F, F)

    def local(i, src, dst):
        return pltpu.make_async_copy(src, dst, r.local_sem.at[i])

    fetch_nf = local(0, r.node_feats, r.nf)
    fetch_tiles = local(1, r.tiles, r.tile_buf)
    fetch_w = local(2, r.weight, r.wv)
    fetch_og = local(3, r.out_grad, r.ogv)
    fetch_nf.start()
    fetch_w.start()
    fetch_og.start()
    fetch_tiles.start()

    eye = lax.broadcasted_iota(jnp.int32, (DOM, DOM), 0) == lax.broadcasted_iota(
        jnp.int32, (DOM, DOM), 1
    )
    for k in range(CUT):
        wide = jnp.broadcast_to(r.sends[k : k + 1, :], (DOM, DOM)).astype(F32)
        col = jnp.sum(jnp.where(eye, wide, 0.0), axis=1, keepdims=True).astype(jnp.int32)
        r.hot[k * DOM : (k + 1) * DOM, :] = (
            col == lax.broadcasted_iota(jnp.int32, (DOM, N), 1)
        ).astype(BF16)
    eye = lax.broadcasted_iota(jnp.int32, (HD, HD), 0) == lax.broadcasted_iota(
        jnp.int32, (HD, HD), 1
    )
    wide = jnp.broadcast_to(r.hub_ids[...], (HD, HD)).astype(F32)
    col = jnp.sum(jnp.where(eye, wide, 0.0), axis=1, keepdims=True).astype(jnp.int32)
    hub_hot = (col == lax.broadcasted_iota(jnp.int32, (HD, N), 1)).astype(BF16)

    def perm(source_of):
        row = lax.broadcasted_iota(jnp.int32, (HALO, HALO), 0)
        lane = lax.broadcasted_iota(jnp.int32, (HALO, HALO), 1)
        return (source_of(row) == lane).astype(BF16)

    def peer_major(i):
        k, zz = mod_(i, CUT), mod_(div_(i, CUT), Z)
        cc, yy = mod_(div_(i, ZC), C), div_(i, ZC * C)
        return k * DOM + (yy * Z + zz) * C + cc

    def z_major(i):
        return (mod_(div_(i, CUT), Y * C) * Z + div_(i, YCC)) * CUT + mod_(i, CUT)

    def yc_major(i):
        return (mod_(div_(i, CUT), Z) * (Y * C) + div_(i, ZC)) * CUT + mod_(i, CUT)

    def to_dom(i):
        yy = div_(i, Z * C * CUT)
        zz = mod_(div_(i, C * CUT), Z)
        return (zz * Y + yy) * (C * CUT) + mod_(i, C * CUT)

    def from_dom(i):
        zz = div_(i, Y * C * CUT)
        yy = mod_(div_(i, C * CUT), Y)
        return (yy * Z + zz) * (C * CUT) + mod_(i, C * CUT)

    fetch_nf.wait()
    r.hub[y, z, c] = dot(hub_hot, r.nf[...]).astype(BF16)
    picked = dot(r.hot[...], r.nf[...]).astype(BF16)
    r.out_halo[...] = dot(perm(peer_major), picked).astype(BF16).reshape(Y * C, ZC, F)
    r.bias8[...] = jnp.broadcast_to(r.bias[...], (8, F))
    pl.semaphore_wait(barrier, Y * C + Z + X - 3)

    done = []

    def exchange(group, src, dst, sems):
        ex = Exchange(group, src, dst, sems)
        done.append(ex)
        return ex

    ex_yc = exchange(gyc, lambda p: r.out_halo.at[p], lambda p: r.st1.at[p], r.s_yc)
    ex_yc.start()
    ex_hz = exchange(gz, lambda p: r.hub.at[y, z, c], lambda p: r.hub.at[y, p, c], r.s_hz)
    ex_hz.start()
    r.st1[yc] = r.out_halo[yc]

    wrows = aligned(c * D, D)
    fetch_w.wait()
    fetch_og.wait()
    ex_xw = exchange(
        gx, lambda p: r.wv.at[wrows], lambda p: r.wfull.at[wrows, cols_of(p)], r.s_xw
    )
    ex_xw.start()
    ex_xs = exchange(
        gx, lambda p: r.nf.at[rows_of(p)], lambda p: r.selfc.at[:, cols_of(p)], r.s_xs
    )
    ex_xs.start()
    ex_xb = exchange(gx, lambda p: r.bias8, lambda p: r.biasc.at[:, cols_of(p)], r.s_xb)
    ex_xb.start()
    ex_xo = exchange(
        gx, lambda p: r.ogv.at[rows_of(p)], lambda p: r.ogc.at[:, cols_of(p)], r.s_xo
    )
    ex_xo.start()
    r.biasc[:, cols_of(x)] = r.bias8[...]
    r.selfc[:, cols_of(x)] = r.nf[rows_of(x), :]
    r.ogc[:, cols_of(x)] = r.ogv[rows_of(x), :]
    r.wfull[:, cols_of(x)] = r.wv[...]

    fetch_tiles.wait()
    r.acc_tiles[0] = jnp.zeros((T, T), BF16)
    r.acc_tiles_t[0] = jnp.zeros((T, T), BF16)

    def add_tile(t, carry):
        value = r.tile_buf[t].astype(F32) + r.acc_tiles[r.prev[t]].astype(F32)
        r.acc_tiles[t + 1] = value.astype(BF16)
        r.acc_tiles_t[t + 1] = value.T.astype(BF16)
        return carry

    lax.fori_loop(0, NT, add_tile, 0)

    ex_yc.wait()
    r.halo_z[...] = (
        dot(perm(z_major), r.st1[...].reshape(HALO, F)).astype(BF16).reshape(Z, YCC, F)
    )
    ex_z = exchange(gz, lambda p: r.halo_z.at[p], lambda p: r.st2.at[p], r.s_z)
    ex_z.start()
    r.st2[z] = r.halo_z[z]

    def place(s, carry):
        for n in range(NB):
            slot = r.last[n * SB + s]
            r.adj[n * T : (n + 1) * T, aligned(s * T, T)] = r.acc_tiles[slot]
            r.adj_t[aligned(s * T, T), n * T : (n + 1) * T] = r.acc_tiles_t[slot]
        return carry

    lax.fori_loop(0, SB, place, 0)

    ex_hz.wait()
    ex_hy = exchange(gy, lambda p: r.hub.at[y, :, c], lambda p: r.hub.at[p, :, c], r.s_hy)
    ex_hy.start()
    hub_to = Relay(other_core, r.s_hc, lambda p: r.hub.at[p, :, c], lambda p: r.hub.at[p, :, c])
    hub_from = Relay(
        other_core, r.s_hc, lambda p: r.hub.at[p, :, 1 - c], lambda p: r.hub.at[p, :, 1 - c]
    )
    hub_to.start(y)

    w_to = Relay(
        other_core,
        r.s_wc,
        lambda p: r.wfull.at[wrows, cols_of(p)],
        lambda p: r.wfull.at[wrows, cols_of(p)],
    )
    other_rows = aligned((1 - c) * D, D)
    w_from = Relay(
        other_core,
        r.s_wc,
        lambda p: r.wfull.at[other_rows, cols_of(p)],
        lambda p: r.wfull.at[other_rows, cols_of(p)],
    )
    def add_deg(n, carry):
        rows = aligned(n * T, T)
        lanes = r.adj[rows, 0:T]
        for s in range(1, SB):
            lanes = lanes + r.adj[rows, s * T : (s + 1) * T]
        r.deg[rows, :] = 1.0 / jnp.maximum(dot(lanes, ones), 1.0)
        return carry

    ones = jnp.ones((T, F), BF16)
    lax.fori_loop(0, NB, add_deg, 0)
    r.acc[...] = dot(r.adj[:, 0:N], r.nf[...])

    def add_hub(p):
        cols = pl.ds(pl.multiple_of(N + HALO + p * PERY, T), PERY)
        r.acc[...] += dot(r.adj[:, cols], r.hub[p].reshape(PERY, F))

    hub_from.copy(y).wait_recv()
    add_hub(y)

    ex_xw.wait_then(w_to.start)
    ex_hy.wait_then(hub_to.start)

    ex_z.wait()
    halo = dot(perm(to_dom), r.st2[...].reshape(HALO, F)).astype(BF16)
    r.acc[...] += dot(r.adj[:, N : N + HALO], halo)

    for i in range(1, Y):
        p = lax.rem(y + i, Y)
        hub_from.copy(p).wait_recv()
        add_hub(p)
    r.mean[...] = (r.acc[...] * r.deg[...]).astype(BF16)
    ex_xm = exchange(
        gx, lambda p: r.mean.at[rows_of(p)], lambda p: r.meanc.at[:, cols_of(p)], r.s_xm
    )
    ex_xm.start()
    r.meanc[:, cols_of(x)] = r.mean[rows_of(x), :]

    ex_xs.wait()
    ex_xb.wait()
    ex_xo.wait()
    gx.each(lambda step, peer: w_from.copy(peer).wait_recv())
    r.pre[...] = dot(r.selfc[...], r.wfull[0:D, :]) + r.biasc[0:1, :]

    for k in range(CUT):
        row = jnp.broadcast_to(r.sends[k : k + 1, :], (N, DOM))
        r.hot_t[:, k * DOM : (k + 1) * DOM] = (
            row == lax.broadcasted_iota(jnp.int32, (N, DOM), 0)
        ).astype(BF16)

    ex_xm.wait()
    pre_act = r.pre[...] + dot(r.meanc[...], r.wfull[D : 2 * D, :])
    sig = jax.nn.sigmoid(pre_act)
    r.gp[...] = (r.ogc[...].astype(F32) * (sig * (1.0 + pre_act * (1.0 - sig)))).astype(BF16)
    r.lo_send[...] = (pre_act * sig).astype(BF16)
    inv_rows = r.deg[rows_of(x), :]
    cat_mean = dot_nt(r.gp[...], r.wfull[D : 2 * D, :])
    for j in range(X):
        r.gm_send[j] = (cat_mean[:, j * F : (j + 1) * F] * inv_rows).astype(BF16)
    ex_xg = exchange(gx, lambda p: r.gm_send.at[p], lambda p: r.gm.at[p], r.s_xg)
    ex_xg.start()
    r.gm[x] = r.gm_send[x]

    for half, src in enumerate((r.selfc, r.meanc)):
        for q in range(0, D, 2 * T):
            part = dot_tn(src[:, q : q + 2 * T], r.gp[...])
            r.wg32[half, q : q + 2 * T, :] = part
            r.wgb[half, q : q + 2 * T, :] = part.astype(BF16)
    ex_gc = exchange(gc, lambda p: r.wgb.at[p], lambda p: r.wg_core.at[p], r.s_gc)
    ex_gc.start()
    bias_sum = jnp.sum(r.gp[...].astype(F32), axis=0, keepdims=True)

    def bias_rows(value):
        full = jnp.broadcast_to(value, (8, F))
        high = full.astype(BF16).astype(F32)
        return jnp.concatenate([high, full - high], axis=0).astype(BF16)

    def bias_of(rows):
        wide = rows.astype(F32)
        return wide[0:8] + wide[8:16]

    cat_self = dot_nt(r.gp[...], r.wfull[0:D, :])
    for j in range(X):
        r.gs_send[j] = cat_self[:, j * F : (j + 1) * F].astype(BF16)
    ex_gc.wait()
    for j in range(X):
        cols = slice(j * F, (j + 1) * F)
        block = r.wg32[c, :, cols] + r.wg_core[1 - c, :, cols].astype(F32)
        r.wx_own[j, 0:D, :] = block
        r.wx_send[j, 0:D, :] = block.astype(BF16)
        r.wx_own[j, D : D + 8, :] = jnp.broadcast_to(bias_sum[:, cols], (8, F))
        r.wx_send[j, D : D + 16, :] = bias_rows(bias_sum[:, cols])
    ex_gx = exchange(gx, lambda p: r.wx_send.at[p], lambda p: r.wx_recv.at[p], r.s_gx)
    ex_gx.start()

    ex_xgs = exchange(gx, lambda p: r.gs_send.at[p], lambda p: r.gs_recv.at[p], r.s_xgs)
    ex_xgs.start()
    ex_xl = exchange(
        gx, lambda p: r.lo_send.at[:, cols_of(p)], lambda p: r.lo_recv.at[p], r.s_xl
    )
    ex_xl.start()
    r.lo_recv[x] = r.lo_send[:, cols_of(x)]
    r.gs_recv[x] = r.gs_send[x]

    ex_xg.wait()
    core_to = Relay(
        other_core, r.s_bhc, lambda p: r.hsb.at[1 - c, p], lambda p: r.hs_core.at[p]
    )
    ex_bhy = exchange(gy, lambda p: r.hy_send.at[p], lambda p: r.hy_recv.at[p], r.s_bhy)

    def spread(rows):
        return dot(r.adj_t[rows, :], r.gm[...].reshape(N, F))

    def back_hub(p):
        rows = spread(pl.ds(pl.multiple_of(N + HALO + p * PERY, T), PERY)).reshape(Z, C, HD, F)
        for cc in range(C):
            r.hs32[cc, p] = rows[:, cc]
            r.hsb[cc, p] = rows[:, cc].astype(BF16)
        core_to.start(p)

    def pair_hub(p, own):
        core_to.copy(p).wait_recv()
        pair = r.hs32[c, p] + r.hs_core[p].astype(F32)
        if own:
            r.hy_own[...] = pair
        else:
            r.hy_send[p] = pair.astype(BF16)
            ex_bhy.start_to(p)

    order = [lax.rem(y + i, Y) for i in range(1, Y)] + [y]
    back_hub(order[0])
    for i in range(1, Y):
        back_hub(order[i])
        pair_hub(order[i - 1], False)

    halo_b = spread(slice(N, N + HALO)).astype(BF16)
    r.halo_zb[...] = dot(perm(from_dom), halo_b).astype(BF16).reshape(Z, YCC, F)
    ex_rz = exchange(gz, lambda p: r.halo_zb.at[p], lambda p: r.rt1.at[p], r.s_rz)
    ex_rz.start()
    r.rt1[z] = r.halo_zb[z]

    pair_hub(y, True)

    r.wx_recv[x] = jnp.zeros((D + 16, F), BF16)
    ex_gx.wait()
    wsum = r.wx_own[x, 0:D, :]
    bsum = r.wx_own[x, D : D + 8, :]
    for j in range(X):
        wsum = wsum + r.wx_recv[j, 0:D, :].astype(F32)
        bsum = bsum + bias_of(r.wx_recv[j, D : D + 16, :])
    for j in range(Y):
        block = wsum[j * DY : (j + 1) * DY]
        r.wy_own[j] = block
        r.wy_send[j, 0:DY, :] = block.astype(BF16)
        r.wy_send[j, DY : DY + 16, :] = bias_rows(bsum[0:1])
    ex_gy = exchange(gy, lambda p: r.wy_send.at[p], lambda p: r.wy_recv.at[p], r.s_gy)
    ex_gy.start()

    r.total[...] = spread(slice(0, N))

    ex_xgs.wait()
    for j in range(X):
        r.total[j * R : (j + 1) * R, :] += r.gs_recv[j].astype(F32)

    r.hy_recv[y] = jnp.zeros((Z, HD, F), BF16)
    ex_bhy.wait()
    hub_y = r.hy_own[...]
    for p in range(Y):
        hub_y = hub_y + r.hy_recv[p].astype(F32)
    r.hy_own[...] = hub_y
    r.hz_send[...] = hub_y.astype(BF16)
    ex_bhz = exchange(gz, lambda p: r.hz_send.at[p], lambda p: r.hz_recv.at[p], r.s_bhz)
    ex_bhz.start()

    ex_rz.wait()
    r.halo_m[...] = (
        dot(perm(yc_major), r.rt1[...].reshape(HALO, F)).astype(BF16).reshape(Y * C, ZC, F)
    )
    ex_ryc = exchange(gyc, lambda p: r.halo_m.at[p], lambda p: r.rt2.at[p], r.s_ryc)
    ex_ryc.start()
    r.rt2[yc] = r.halo_m[yc]

    r.wy_recv[y] = jnp.zeros((DY + 16, F), BF16)
    ex_gy.wait()
    wsum = r.wy_own[y]
    for j in range(Y):
        wsum = wsum + r.wy_recv[j, 0:DY, :].astype(F32)
        bsum = bsum + bias_of(r.wy_recv[j, DY : DY + 16, :])
    for j in range(Z):
        r.wz_send[j, 0:DZ, :] = wsum[j * DZ : (j + 1) * DZ]
        r.wz_send[j, DZ : DZ + 8, :] = bsum
    ex_gz = exchange(gz, lambda p: r.wz_send.at[p], lambda p: r.wz_recv.at[p], r.s_gz)
    ex_gz.start()

    ex_xl.wait()
    lo_out = local(5, r.lo_recv, r.layer_out)
    lo_out.start()

    ex_ryc.wait()
    returned = dot(perm(from_peer_major(dims)), r.rt2[...].reshape(HALO, F)).astype(BF16)
    r.total[...] += dot(r.hot_t[...], returned)

    r.wz_recv[z] = jnp.zeros((DZ + 8, F), F32)
    ex_gz.wait()
    zsum = (jnp.sum(r.wz_recv[...], axis=0) + r.wz_send[z]) * scale
    r.wout[z] = zsum[0:DZ]
    r.bias_core[c] = zsum[DZ : DZ + 8]
    ex_az = exchange(gz, lambda p: r.wout.at[z], lambda p: r.wout.at[p], r.s_az)
    ex_az.start()
    ex_bc = exchange(gc, lambda p: r.bias_core.at[c], lambda p: r.bias_core.at[p], r.s_bc)
    ex_bc.start()

    r.hz_recv[z] = jnp.zeros((HD, F), BF16)
    ex_bhz.wait()
    hub_mine = r.hy_own[z] + jnp.sum(r.hz_recv[...].astype(F32), axis=0)
    high = hub_mine.astype(BF16)
    low = (hub_mine - high.astype(F32)).astype(BF16)
    hub_hot_t = (
        jnp.broadcast_to(r.hub_ids[...], (N, HD)) == lax.broadcasted_iota(jnp.int32, (N, HD), 0)
    ).astype(BF16)
    r.ng[...] = (r.total[...] + dot(hub_hot_t, high) + dot(hub_hot_t, low)).astype(BF16)
    ng_out = local(6, r.ng, r.node_grad)
    ng_out.start()

    ex_az.wait()
    r.wb_all[yc_row(c, Y, y)] = r.wout[...].reshape(DY, F).astype(BF16)
    ex_ay = exchange(
        gyc,
        lambda p: r.wb_all.at[yc_row(c, Y, y)],
        lambda p: r.wb_all.at[yc_row(lax.rem(p, C), Y, lax.div(p, C))],
        r.s_ay,
    )
    ex_ay.start()
    ex_bc.wait()
    r.bias_grad[...] = r.bias_core[0, 0:1] + r.bias_core[1, 0:1]
    ex_ay.wait()
    r.wg_all[...] = r.wb_all[...].astype(F32).reshape(C * Y, Z, DZ, F)
    r.wg_all[yc_row(c, Y, y)] = r.wout[...]

    w_out = local(7, r.wg_all, r.weight_grad)
    w_out.start()
    lo_out.wait()
    ng_out.wait()
    w_out.wait()
    for ex in done:
        ex.drain()
    for p in range(Y):
        hub_to.copy(p).wait_send()
        core_to.copy(p).wait_send()
    gx.each(lambda step, peer: w_to.copy(peer).wait_send())


def yc_row(c, Y, y):
    return c * Y + y


def from_peer_major(dims):
    Y, Z, C, CUT = dims[0], dims[1], dims[2], dims[9]
    DOM = Y * Z * C

    def source(i):
        k, q = div_(i, DOM), mod_(i, DOM)
        cc, zz, yy = mod_(q, C), mod_(div_(q, C), Z), div_(q, C * Z)
        return ((yy * C + cc) * Z + zz) * CUT + k

    return source


def copy_kernel(*refs):
    n = len(refs) // 2
    for src, dst in zip(refs[:n], refs[n:]):
        dst[...] = src[...]


def per_device(
    sizes,
    node_feats,
    neigh_weight,
    bias,
    out_grad,
    tile_values,
    tile_src,
    tile_dst,
    tile_count,
    hub_rows,
    send_rows,
):
    Y, Z, C, X = sizes
    N, F = node_feats.shape
    NT, T = tile_values.shape[:2]
    CUT = send_rows.shape[1]
    HD = hub_rows.shape[0]
    DOM = Y * Z * C
    HALO = DOM * CUT
    NB, SB = N // T, (N + HALO + DOM * HD) // T
    D, R = X * F, N // X
    ZC, YCC = Z * CUT, Y * C * CUT
    DY = D // Y
    DZ = DY // Z

    at = jnp.arange(NT, dtype=jnp.int32)
    key = jnp.where(at < tile_count[0], tile_dst * SB + tile_src, -1)
    same = (key[:, None] == key[None, :]) & (at[None, :] < at[:, None])
    prev = jnp.max(jnp.where(same, at[None, :] + 1, 0), axis=1)
    place = jnp.arange(NB * SB, dtype=jnp.int32)
    last = jnp.max(jnp.where(place[:, None] == key[None, :], at[None, :] + 1, 0), axis=1)

    dims = (Y, Z, C, X, N, T, NT, F, HD, CUT, 1.0 / math.sqrt(N * DOM))
    vm = pl.BlockSpec(memory_space=pltpu.VMEM)
    sm = pl.BlockSpec(memory_space=pltpu.SMEM)
    hbm = pl.BlockSpec(memory_space=pl.ANY)

    def b(*shape):
        return pltpu.VMEM(shape, BF16)

    def f(*shape):
        return pltpu.VMEM(shape, F32)

    def sem(n):
        return pltpu.SemaphoreType.DMA((2, n))

    inputs = dict(
        node_feats=(node_feats, hbm),
        weight=(neigh_weight, hbm),
        out_grad=(out_grad, hbm),
        tiles=(tile_values, hbm),
        bias=(bias[None, :], vm),
        sends=(send_rows.T, vm),
        hub_ids=(hub_rows[None, :], vm),
        prev=(prev, sm),
        last=(last, sm),
    )
    outputs = dict(
        layer_out=(jax.ShapeDtypeStruct((X, R, F), BF16), hbm),
        node_grad=(jax.ShapeDtypeStruct((N, F), BF16), hbm),
        weight_grad=(jax.ShapeDtypeStruct((C * Y, Z, DZ, F), F32), hbm),
        bias_grad=(jax.ShapeDtypeStruct((1, F), F32), vm),
    )
    scratch = dict(
        nf=b(N, F),
        tile_buf=b(NT, T, T),
        acc_tiles=b(NT + 1, T, T),
        acc_tiles_t=b(NT + 1, T, T),
        adj=b(N, SB * T),
        adj_t=b(SB * T, N),
        hot=b(HALO, N),
        hot_t=b(N, HALO),
        out_halo=b(Y * C, ZC, F),
        st1=b(Y * C, ZC, F),
        st2=b(Z, YCC, F),
        halo_z=b(Z, YCC, F),
        hub=b(Y, Z, C, HD, F),
        deg=f(N, F),
        acc=f(N, F),
        selfc=b(R, D),
        meanc=b(R, D),
        ogc=b(R, D),
        wfull=b(2 * D, D),
        bias8=f(8, F),
        biasc=f(8, D),
        mean=b(N, F),
        pre=f(R, D),
        lo_send=b(R, D),
        lo_recv=b(X, R, F),
        wv=b(2 * D, F),
        ogv=b(N, F),
        wg_all=f(C * Y, Z, DZ, F),
        wb_all=b(C * Y, DY, F),
        gp=b(R, D),
        gm_send=b(X, R, F),
        gm=b(X, R, F),
        gs_send=b(X, R, F),
        gs_recv=b(X, R, F),
        wg32=f(C, D, D),
        wgb=b(C, D, D),
        wg_core=b(C, D, D),
        wx_send=b(X, D + 16, F),
        wx_recv=b(X, D + 16, F),
        wx_own=f(X, D + 8, F),
        wy_send=b(Y, DY + 16, F),
        wy_recv=b(Y, DY + 16, F),
        wy_own=f(Y, DY, F),
        wz_send=f(Z, DZ + 8, F),
        wz_recv=f(Z, DZ + 8, F),
        wout=f(Z, DZ, F),
        bias_core=f(C, 8, F),
        hs32=f(C, Y, Z, HD, F),
        hsb=b(C, Y, Z, HD, F),
        hs_core=b(Y, Z, HD, F),
        hy_send=b(Y, Z, HD, F),
        hy_recv=b(Y, Z, HD, F),
        hy_own=f(Z, HD, F),
        hz_send=b(Z, HD, F),
        hz_recv=b(Z, HD, F),
        halo_zb=b(Z, YCC, F),
        rt1=b(Z, YCC, F),
        halo_m=b(Y * C, ZC, F),
        rt2=b(Y * C, ZC, F),
        total=f(N, F),
        ng=b(N, F),
        local_sem=pltpu.SemaphoreType.DMA((8,)),
        s_yc=sem(Y * C),
        s_z=sem(Z),
        s_hz=sem(Z),
        s_hy=sem(Y),
        s_hc=sem(Y),
        s_xs=sem(X),
        s_xo=sem(X),
        s_xw=sem(X),
        s_xb=sem(X),
        s_wc=sem(X),
        s_xm=sem(X),
        s_xl=sem(X),
        s_xg=sem(X),
        s_xgs=sem(X),
        s_gc=sem(C),
        s_gx=sem(X),
        s_gy=sem(Y),
        s_gz=sem(Z),
        s_az=sem(Z),
        s_ay=sem(Y * C),
        s_bc=sem(C),
        s_bhc=sem(Y),
        s_bhy=sem(Y),
        s_bhz=sem(Z),
        s_rz=sem(Z),
        s_ryc=sem(Y * C),
    )
    names = list(inputs) + list(outputs) + list(scratch)
    results = pl.pallas_call(
        functools.partial(kernel, dims, names),
        out_shape=[shape for shape, _ in outputs.values()],
        in_specs=[spec for _, spec in inputs.values()],
        out_specs=[spec for _, spec in outputs.values()],
        scratch_shapes=list(scratch.values()),
        compiler_params=pltpu.CompilerParams(
            collective_id=0, has_side_effects=True, vmem_limit_bytes=60 * 1024 * 1024
        ),
    )(*[array for array, _ in inputs.values()])
    layer_out, node_grad, weight_grad, bias_grad = pl.pallas_call(
        copy_kernel,
        out_shape=[jax.ShapeDtypeStruct(v.shape, v.dtype) for v in results],
        in_specs=[vm] * 4,
        out_specs=[vm] * 4,
    )(*results)
    return (
        layer_out.reshape(N, F),
        node_grad,
        weight_grad.reshape(2 * D, F),
        bias_grad.reshape(F),
    )


def solution(mesh, y_chips=Y_CHIPS):
    dom, feat = mesh.shape["dom"], mesh.shape["feat"]
    sizes = (y_chips, dom // (CORES * y_chips), CORES, feat)
    in_specs = (
        P("dom", "feat"),
        P(None, "feat"),
        P("feat"),
        P("dom", "feat"),
        P("dom", None, None),
        P("dom"),
        P("dom"),
        P("dom"),
        P("dom"),
        P("dom", None),
    )
    out_specs = (P("dom", "feat"), P("dom", "feat"), P(None, "feat"), P("feat"))
    return jax.shard_map(
        functools.partial(per_device, sizes),
        mesh=mesh,
        in_specs=in_specs,
        out_specs=out_specs,
        check_vma=False,
    )
```

```python
import functools
import math
import types

import jax
import jax.numpy as jnp
from jax import lax
from jax.experimental import pallas as pl
from jax.experimental.pallas import tpu as pltpu
from jax.sharding import PartitionSpec as P

BF16 = jnp.bfloat16
F32 = jnp.float32
CORES = 2
Y_CHIPS = 4


def dot(a, b):
    return jnp.dot(a, b, preferred_element_type=F32)


def dot_nt(a, b):
    return lax.dot_general(a, b, (((1,), (1,)), ((), ())), preferred_element_type=F32)


def dot_tn(a, b):
    return lax.dot_general(a, b, (((0,), (0,)), ((), ())), preferred_element_type=F32)


class Group:
    def __init__(self, size, me, device):
        self.size, self.me, self.device = size, me, device

    def each(self, body):
        for step in range(1, self.size):
            body((self.me + step) & (self.size - 1))


class Exchange:
    def __init__(self, group, src, dst, sems, sent, landed, each=False):
        self.group, self.src, self.dst, self.sems = group, src, dst, sems
        self.sent, self.landed, self.one_by_one = sent, landed, each

    def copy(self, peer, landing):
        return pltpu.make_async_remote_copy(
            src_ref=self.src(peer),
            dst_ref=self.dst(landing),
            send_sem=self.sems.at[0, 0],
            recv_sem=self.sems.at[1, landing if self.one_by_one else 0],
            device_id=self.group.device(peer),
            device_id_type=pl.DeviceIdType.MESH,
        )

    def all(self, part):
        return pltpu.make_async_remote_copy(
            src_ref=part,
            dst_ref=part,
            send_sem=self.sems.at[0, 0],
            recv_sem=self.sems.at[1, 0],
            device_id=self.group.device((self.group.me + 1) & (self.group.size - 1)),
            device_id_type=pl.DeviceIdType.MESH,
        )

    def start_to(self, peer):
        self.copy(peer, self.group.me).start()

    def start(self):
        self.group.each(self.start_to)

    def wait(self):
        self.all(self.landed).wait_recv()

    def wait_then(self, after):
        def body(peer):
            self.copy(peer, peer).wait_recv()
            after(peer)

        self.group.each(body)

    def drain(self):
        self.all(self.sent).wait_send()


class Relay:
    def __init__(self, device, sems, src, dst):
        self.device, self.sems, self.src, self.dst = device, sems, src, dst

    def copy(self, slot):
        return pltpu.make_async_remote_copy(
            src_ref=self.src(slot),
            dst_ref=self.dst(slot),
            send_sem=self.sems.at[0, slot],
            recv_sem=self.sems.at[1, slot],
            device_id=self.device,
            device_id_type=pl.DeviceIdType.MESH,
        )

    def start(self, slot):
        self.copy(slot).start()


def log2(n):
    return n.bit_length() - 1


def div_(a, n):
    return lax.shift_right_logical(a, log2(n))


def mod_(a, n):
    return a & (n - 1)


def aligned(start, size):
    return pl.ds(pl.multiple_of(start, size), size)


def kernel(dims, names, *refs):
    r = types.SimpleNamespace(**dict(zip(names, refs)))
    Y, Z, C, X, N, T, NT, F, HD, CUT, scale = dims
    D = X * F
    R = N // X
    DOM = Y * Z * C
    HALO = DOM * CUT
    NB = N // T
    SB = (N + HALO + DOM * HD) // T
    ZC, YCC = Z * CUT, Y * C * CUT
    PERY = Z * C * HD
    DY = D // Y
    DZ = DY // Z
    dom, x = lax.axis_index("dom"), lax.axis_index("feat")
    c = dom & (C - 1)
    z = (dom >> log2(C)) & (Z - 1)
    y = dom >> log2(C * Z)
    yc = y * C + c

    def at(yy, zz, cc):
        return ((yy * Z + zz) * C + cc, x)

    gyc = Group(Y * C, yc, lambda p: at(p >> log2(C), z, p & (C - 1)))
    gz = Group(Z, z, lambda p: at(y, p, c))
    gy = Group(Y, y, lambda p: at(p, z, c))
    gc = Group(C, c, lambda p: at(y, z, p))
    gx = Group(X, x, lambda p: (dom, p))
    other_core = at(y, z, 1 - c)

    barrier = pltpu.get_barrier_semaphore()
    for group in (gyc, gz, gx):
        group.each(
            lambda peer, group=group: pl.semaphore_signal(
                barrier, inc=1, device_id=group.device(peer), device_id_type=pl.DeviceIdType.MESH
            )
        )

    def rows_of(p):
        return aligned(p * R, R)

    def cols_of(p):
        return aligned(p * F, F)

    def local(i, src, dst):
        return pltpu.make_async_copy(src, dst, r.local_sem.at[i])

    fetch_nf = local(0, r.node_feats, r.nf)
    fetch_tiles = local(1, r.tiles, r.tile_buf)
    fetch_w = local(2, r.weight, r.wv)
    fetch_og = local(3, r.out_grad, r.ogv)
    fetch_nf.start()
    fetch_w.start()
    fetch_og.start()
    fetch_tiles.start()

    eye = lax.broadcasted_iota(jnp.int32, (DOM, DOM), 0) == lax.broadcasted_iota(
        jnp.int32, (DOM, DOM), 1
    )
    for k in range(CUT):
        wide = jnp.broadcast_to(r.sends[k : k + 1, :], (DOM, DOM)).astype(F32)
        col = jnp.sum(jnp.where(eye, wide, 0.0), axis=1, keepdims=True).astype(jnp.int32)
        r.hot[k * DOM : (k + 1) * DOM, :] = (
            col == lax.broadcasted_iota(jnp.int32, (DOM, N), 1)
        ).astype(BF16)
    eye = lax.broadcasted_iota(jnp.int32, (HD, HD), 0) == lax.broadcasted_iota(
        jnp.int32, (HD, HD), 1
    )
    wide = jnp.broadcast_to(r.hub_ids[...], (HD, HD)).astype(F32)
    col = jnp.sum(jnp.where(eye, wide, 0.0), axis=1, keepdims=True).astype(jnp.int32)
    hub_hot = (col == lax.broadcasted_iota(jnp.int32, (HD, N), 1)).astype(BF16)

    def perm(source_of):
        row = lax.broadcasted_iota(jnp.int32, (HALO, HALO), 0)
        lane = lax.broadcasted_iota(jnp.int32, (HALO, HALO), 1)
        return (source_of(row) == lane).astype(BF16)

    def peer_major(i):
        k, zz = mod_(i, CUT), mod_(div_(i, CUT), Z)
        cc, yy = mod_(div_(i, ZC), C), div_(i, ZC * C)
        return k * DOM + (yy * Z + zz) * C + cc

    def z_major(i):
        return (mod_(div_(i, CUT), Y * C) * Z + div_(i, YCC)) * CUT + mod_(i, CUT)

    def yc_major(i):
        return (mod_(div_(i, CUT), Z) * (Y * C) + div_(i, ZC)) * CUT + mod_(i, CUT)

    def to_dom(i):
        yy = div_(i, Z * C * CUT)
        zz = mod_(div_(i, C * CUT), Z)
        return (zz * Y + yy) * (C * CUT) + mod_(i, C * CUT)

    def from_dom(i):
        zz = div_(i, Y * C * CUT)
        yy = mod_(div_(i, C * CUT), Y)
        return (yy * Z + zz) * (C * CUT) + mod_(i, C * CUT)

    fetch_nf.wait()
    r.hub[y, z, c] = dot(hub_hot, r.nf[...]).astype(BF16)
    picked = dot(r.hot[...], r.nf[...]).astype(BF16)
    r.out_halo[...] = dot(perm(peer_major), picked).astype(BF16).reshape(Y * C, ZC, F)
    r.bias8[...] = jnp.broadcast_to(r.bias[...], (8, F))
    pl.semaphore_wait(barrier, Y * C + Z + X - 3)

    done = []

    def most(ref):
        return ref.at[pl.ds(0, ref.shape[0] - 1)]

    def cols3(ref):
        return ref.at[:, 0 : D - F]


    def exchange(group, src, dst, sems, sent, landed, each=False):
        ex = Exchange(group, src, dst, sems, sent, landed, each)
        done.append(ex)
        return ex

    ex_yc = exchange(
        gyc, lambda p: r.out_halo.at[p], lambda p: r.st1.at[p],
        r.s_yc,
        most(r.out_halo),
        most(r.st1),
    )
    ex_yc.start()
    ex_hz = exchange(
        gz, lambda p: r.hub.at[y, z, c], lambda p: r.hub.at[y, p, c],
        r.s_hz,
        r.hub.at[y, pl.ds(0, Z - 1), c],
        r.hub.at[y, pl.ds(0, Z - 1), c],
    )
    ex_hz.start()
    r.st1[yc] = r.out_halo[yc]

    wrows = aligned(c * D, D)
    fetch_w.wait()
    fetch_og.wait()
    ex_xw = exchange(
        gx, lambda p: r.wv.at[wrows], lambda p: r.wfull.at[wrows, cols_of(p)],
        r.s_xw,
        r.wfull.at[wrows, 0 : D - F],
        r.wfull.at[wrows, 0 : D - F],
        each=True,
    )
    ex_xw.start()
    ex_xs = exchange(
        gx, lambda p: r.nf.at[rows_of(p)], lambda p: r.selfc.at[:, cols_of(p)],
        r.s_xs,
        cols3(r.selfc),
        cols3(r.selfc),
    )
    ex_xs.start()
    ex_xb = exchange(
        gx, lambda p: r.bias8, lambda p: r.biasc.at[:, cols_of(p)],
        r.s_xb,
        cols3(r.biasc),
        cols3(r.biasc),
    )
    ex_xb.start()
    ex_xo = exchange(
        gx, lambda p: r.ogv.at[rows_of(p)], lambda p: r.ogc.at[:, cols_of(p)],
        r.s_xo,
        cols3(r.ogc),
        cols3(r.ogc),
    )
    ex_xo.start()
    r.biasc[:, cols_of(x)] = r.bias8[...]
    r.selfc[:, cols_of(x)] = r.nf[rows_of(x), :]
    r.ogc[:, cols_of(x)] = r.ogv[rows_of(x), :]
    r.wfull[:, cols_of(x)] = r.wv[...]

    fetch_tiles.wait()
    turn = NT // 8 if NT % 8 == 0 else 1

    def turn_tiles(i, carry):
        for k in range(NT // turn):
            t = i * (NT // turn) + k
            r.turned[t] = r.tile_buf[t].T
        return carry

    lax.fori_loop(0, turn, turn_tiles, 0)
    r.acc_tiles_t[0] = jnp.zeros((T, T), BF16)

    def add_tile(t, carry):
        r.acc_tiles_t[t + 1] = r.turned[t] + r.acc_tiles_t[r.prev[t]]
        return carry

    lax.fori_loop(0, NT, add_tile, 0)

    ex_yc.wait()
    r.halo_z[...] = (
        dot(perm(z_major), r.st1[...].reshape(HALO, F)).astype(BF16).reshape(Z, YCC, F)
    )
    ex_z = exchange(
        gz, lambda p: r.halo_z.at[p], lambda p: r.st2.at[p],
        r.s_z,
        most(r.halo_z),
        most(r.st2),
    )
    ex_z.start()
    r.st2[z] = r.halo_z[z]

    ex_hz.wait()
    ex_hy = exchange(
        gy, lambda p: r.hub.at[y, :, c], lambda p: r.hub.at[p, :, c],
        r.s_hy,
        r.hub.at[pl.ds(0, Y - 1), :, c],
        r.hub.at[pl.ds(0, Y - 1), :, c],
        each=True,
    )
    ex_hy.start()
    hub_to = Relay(other_core, r.s_hc, lambda p: r.hub.at[p, :, c], lambda p: r.hub.at[p, :, c])
    hub_from = Relay(
        other_core, r.s_hc, lambda p: r.hub.at[p, :, 1 - c], lambda p: r.hub.at[p, :, 1 - c]
    )
    hub_to.start(y)

    w_to = Relay(
        other_core,
        r.s_wc,
        lambda p: r.wfull.at[wrows, cols_of(p)],
        lambda p: r.wfull.at[wrows, cols_of(p)],
    )
    other_rows = aligned((1 - c) * D, D)
    w_from = Relay(
        other_core,
        r.s_wc,
        lambda p: r.wfull.at[other_rows, cols_of(p)],
        lambda p: r.wfull.at[other_rows, cols_of(p)],
    )
    def place(s, carry):
        for n in range(NB):
            r.adj_t[aligned(s * T, T), n * T : (n + 1) * T] = r.acc_tiles_t[r.last[n * SB + s]]
        return carry

    lax.fori_loop(0, SB, place, 0)

    def gather(rows, source):
        ones = jnp.ones((16, source.shape[0]), BF16)
        return dot(jnp.concatenate([source.T, ones], axis=0), r.adj_t[rows, :])

    def add_hub(p):
        rows = pl.ds(pl.multiple_of(N + HALO + p * PERY, T), PERY)
        r.acc[...] += gather(rows, r.hub[p].reshape(PERY, F))

    r.acc[...] = gather(slice(0, N), r.nf[...])
    hub_from.copy(y).wait_recv()
    add_hub(y)

    ex_xw.wait_then(w_to.start)
    ex_hy.wait_then(hub_to.start)

    ex_z.wait()
    halo = dot(perm(to_dom), r.st2[...].reshape(HALO, F)).astype(BF16)
    r.acc[...] += gather(slice(N, N + HALO), halo)

    for i in range(1, Y):
        p = (y + i) & (Y - 1)
        hub_from.copy(p).wait_recv()
        add_hub(p)
    r.inv[...] = 1.0 / jnp.maximum(r.acc[F : F + 8, :], 1.0)
    r.mean[...] = (r.acc[0:F, :] * r.inv[0:1, :]).astype(BF16).T
    ex_xm = exchange(
        gx, lambda p: r.mean.at[rows_of(p)], lambda p: r.meanc.at[:, cols_of(p)],
        r.s_xm,
        cols3(r.meanc),
        cols3(r.meanc),
    )
    ex_xm.start()
    r.meanc[:, cols_of(x)] = r.mean[rows_of(x), :]

    ex_xs.wait()
    ex_xb.wait()
    ex_xo.wait()
    gx.each(lambda peer: w_from.copy(peer).wait_recv())
    r.pre[...] = dot(r.selfc[...], r.wfull[0:D, :]) + r.biasc[0:1, :]

    for k in range(CUT):
        row = jnp.broadcast_to(r.sends[k : k + 1, :], (N, DOM))
        r.hot_t[:, k * DOM : (k + 1) * DOM] = (
            row == lax.broadcasted_iota(jnp.int32, (N, DOM), 0)
        ).astype(BF16)

    inv_rows = jnp.broadcast_to(r.inv[0:1, rows_of(x)], (F, R)).T
    ex_xm.wait()
    pre_act = r.pre[...] + dot(r.meanc[...], r.wfull[D : 2 * D, :])
    sig = jax.nn.sigmoid(pre_act)
    r.gp[...] = (r.ogc[...].astype(F32) * (sig * (1.0 + pre_act * (1.0 - sig)))).astype(BF16)
    r.lo_send[...] = (pre_act * sig).astype(BF16)
    cat_mean = dot_nt(r.gp[...], r.wfull[D : 2 * D, :])
    for j in range(X):
        r.gm_send[j] = (cat_mean[:, j * F : (j + 1) * F] * inv_rows).astype(BF16)
    ex_xg = exchange(
        gx, lambda p: r.gm_send.at[p], lambda p: r.gm.at[p],
        r.s_xg,
        most(r.gm_send),
        most(r.gm),
    )
    ex_xg.start()
    r.gm[x] = r.gm_send[x]

    for half, src in enumerate((r.selfc, r.meanc)):
        for q in range(0, D, 2 * T):
            part = dot_tn(src[:, q : q + 2 * T], r.gp[...])
            r.wg32[half, q : q + 2 * T, :] = part
            r.wgb[half, q : q + 2 * T, :] = part.astype(BF16)
    ex_gc = exchange(
        gc, lambda p: r.wgb.at[p], lambda p: r.wg_core.at[p],
        r.s_gc,
        most(r.wgb),
        most(r.wg_core),
    )
    ex_gc.start()
    bias_sum = jnp.sum(r.gp[...].astype(F32), axis=0, keepdims=True)

    def bias_rows(value):
        full = jnp.broadcast_to(value, (8, F))
        high = full.astype(BF16).astype(F32)
        return jnp.concatenate([high, full - high], axis=0).astype(BF16)

    def bias_of(rows):
        wide = rows.astype(F32)
        return wide[0:8] + wide[8:16]

    cat_self = dot_nt(r.gp[...], r.wfull[0:D, :])
    for j in range(X):
        r.gs_send[j] = cat_self[:, j * F : (j + 1) * F].astype(BF16)
    ex_gc.wait()
    for j in range(X):
        cols = slice(j * F, (j + 1) * F)
        block = r.wg32[c, :, cols] + r.wg_core[1 - c, :, cols].astype(F32)
        r.wx_own[j, 0:D, :] = block
        r.wx_send[j, 0:D, :] = block.astype(BF16)
        r.wx_own[j, D : D + 8, :] = jnp.broadcast_to(bias_sum[:, cols], (8, F))
        r.wx_send[j, D : D + 16, :] = bias_rows(bias_sum[:, cols])
    ex_gx = exchange(
        gx, lambda p: r.wx_send.at[p], lambda p: r.wx_recv.at[p],
        r.s_gx,
        most(r.wx_send),
        most(r.wx_recv),
    )
    ex_gx.start()

    ex_xgs = exchange(
        gx, lambda p: r.gs_send.at[p], lambda p: r.gs_recv.at[p],
        r.s_xgs,
        most(r.gs_send),
        most(r.gs_recv),
    )
    ex_xgs.start()
    ex_xl = exchange(
        gx, lambda p: r.lo_send.at[:, cols_of(p)], lambda p: r.lo_recv.at[p],
        r.s_xl,
        cols3(r.lo_send),
        most(r.lo_recv),
    )
    ex_xl.start()
    r.lo_recv[x] = r.lo_send[:, cols_of(x)]
    r.gs_recv[x] = r.gs_send[x]

    ex_xg.wait()
    core_to = Relay(
        other_core, r.s_bhc, lambda p: r.hsb.at[1 - c, p], lambda p: r.hs_core.at[p]
    )
    ex_bhy = exchange(
        gy, lambda p: r.hy_send.at[p], lambda p: r.hy_recv.at[p],
        r.s_bhy,
        most(r.hy_send),
        most(r.hy_recv),
    )

    def spread(rows):
        return dot(r.adj_t[rows, :], r.gm[...].reshape(N, F))

    def back_hub(p):
        rows = spread(pl.ds(pl.multiple_of(N + HALO + p * PERY, T), PERY)).reshape(Z, C, HD, F)
        for cc in range(C):
            r.hs32[cc, p] = rows[:, cc]
            r.hsb[cc, p] = rows[:, cc].astype(BF16)
        core_to.start(p)

    def pair_hub(p, own):
        core_to.copy(p).wait_recv()
        pair = r.hs32[c, p] + r.hs_core[p].astype(F32)
        if own:
            r.hy_own[...] = pair
        else:
            r.hy_send[p] = pair.astype(BF16)
            ex_bhy.start_to(p)

    order = [(y + i) & (Y - 1) for i in range(1, Y)] + [y]
    back_hub(order[0])
    for i in range(1, Y):
        back_hub(order[i])
        pair_hub(order[i - 1], False)

    halo_b = spread(slice(N, N + HALO)).astype(BF16)
    r.halo_zb[...] = dot(perm(from_dom), halo_b).astype(BF16).reshape(Z, YCC, F)
    ex_rz = exchange(
        gz, lambda p: r.halo_zb.at[p], lambda p: r.rt1.at[p],
        r.s_rz,
        most(r.halo_zb),
        most(r.rt1),
    )
    ex_rz.start()
    r.rt1[z] = r.halo_zb[z]

    pair_hub(y, True)

    r.wx_recv[x] = jnp.zeros((D + 16, F), BF16)
    ex_gx.wait()
    wsum = r.wx_own[x, 0:D, :]
    bsum = r.wx_own[x, D : D + 8, :]
    for j in range(X):
        wsum = wsum + r.wx_recv[j, 0:D, :].astype(F32)
        bsum = bsum + bias_of(r.wx_recv[j, D : D + 16, :])
    for j in range(Y):
        block = wsum[j * DY : (j + 1) * DY]
        r.wy_own[j] = block
        r.wy_send[j, 0:DY, :] = block.astype(BF16)
        r.wy_send[j, DY : DY + 16, :] = bias_rows(bsum[0:1])
    ex_gy = exchange(
        gy, lambda p: r.wy_send.at[p], lambda p: r.wy_recv.at[p],
        r.s_gy,
        most(r.wy_send),
        most(r.wy_recv),
    )
    ex_gy.start()

    r.total[...] = spread(slice(0, N))

    ex_xgs.wait()
    for j in range(X):
        r.total[j * R : (j + 1) * R, :] += r.gs_recv[j].astype(F32)

    r.wy_recv[y] = jnp.zeros((DY + 16, F), BF16)
    ex_gy.wait()
    wsum = r.wy_own[y]
    for j in range(Y):
        wsum = wsum + r.wy_recv[j, 0:DY, :].astype(F32)
        bsum = bsum + bias_of(r.wy_recv[j, DY : DY + 16, :])
    for j in range(Z):
        r.wz_send[j, 0:DZ, :] = wsum[j * DZ : (j + 1) * DZ]
        r.wz_send[j, DZ : DZ + 8, :] = bsum
    ex_gz = exchange(
        gz, lambda p: r.wz_send.at[p], lambda p: r.wz_recv.at[p],
        r.s_gz,
        most(r.wz_send),
        most(r.wz_recv),
    )
    ex_gz.start()

    r.hy_recv[y] = jnp.zeros((Z, HD, F), BF16)
    ex_bhy.wait()
    hub_y = r.hy_own[...]
    for p in range(Y):
        hub_y = hub_y + r.hy_recv[p].astype(F32)
    r.hy_own[...] = hub_y
    r.hz_send[...] = hub_y.astype(BF16)
    ex_bhz = exchange(
        gz, lambda p: r.hz_send.at[p], lambda p: r.hz_recv.at[p],
        r.s_bhz,
        most(r.hz_send),
        most(r.hz_recv),
    )
    ex_bhz.start()

    ex_rz.wait()
    r.halo_m[...] = (
        dot(perm(yc_major), r.rt1[...].reshape(HALO, F)).astype(BF16).reshape(Y * C, ZC, F)
    )
    ex_ryc = exchange(
        gyc, lambda p: r.halo_m.at[p], lambda p: r.rt2.at[p],
        r.s_ryc,
        most(r.halo_m),
        most(r.rt2),
    )
    ex_ryc.start()
    r.rt2[yc] = r.halo_m[yc]

    r.wz_recv[z] = jnp.zeros((DZ + 8, F), F32)
    ex_gz.wait()
    zsum = (jnp.sum(r.wz_recv[...], axis=0) + r.wz_send[z]) * scale
    r.wout[z] = zsum[0:DZ]
    r.bias_core[c] = zsum[DZ : DZ + 8]
    ex_az = exchange(
        gz, lambda p: r.wout.at[z], lambda p: r.wout.at[p],
        r.s_az,
        most(r.wout),
        most(r.wout),
    )
    ex_az.start()
    ex_bc = exchange(
        gc, lambda p: r.bias_core.at[c], lambda p: r.bias_core.at[p],
        r.s_bc,
        most(r.bias_core),
        most(r.bias_core),
    )
    ex_bc.start()

    ex_xl.wait()
    lo_out = local(5, r.lo_recv, r.layer_out)
    lo_out.start()

    ex_ryc.wait()
    returned = dot(perm(from_peer_major(dims)), r.rt2[...].reshape(HALO, F)).astype(BF16)
    r.total[...] += dot(r.hot_t[...], returned)

    r.hz_recv[z] = jnp.zeros((HD, F), BF16)
    ex_bhz.wait()
    hub_mine = r.hy_own[z] + jnp.sum(r.hz_recv[...].astype(F32), axis=0)
    high = hub_mine.astype(BF16)
    low = (hub_mine - high.astype(F32)).astype(BF16)
    hub_hot_t = (
        jnp.broadcast_to(r.hub_ids[...], (N, HD)) == lax.broadcasted_iota(jnp.int32, (N, HD), 0)
    ).astype(BF16)
    r.ng[...] = (r.total[...] + dot(hub_hot_t, high) + dot(hub_hot_t, low)).astype(BF16)
    ng_out = local(6, r.ng, r.node_grad)
    ng_out.start()

    ex_az.wait()
    r.wb_all[yc_row(c, Y, y)] = r.wout[...].reshape(DY, F).astype(BF16)
    ex_ay = exchange(
        gyc,
        lambda p: r.wb_all.at[yc_row(c, Y, y)],
        lambda p: r.wb_all.at[yc_row(p & (C - 1), Y, p >> log2(C))],
        r.s_ay,
        most(r.wb_all),
        most(r.wb_all),
    )
    ex_ay.start()
    ex_bc.wait()
    r.bias_grad[...] = r.bias_core[0, 0:1] + r.bias_core[1, 0:1]
    ex_ay.wait()
    r.wg_all[...] = r.wb_all[...].astype(F32).reshape(C * Y, Z, DZ, F)
    r.wg_all[yc_row(c, Y, y)] = r.wout[...]

    w_out = local(7, r.wg_all, r.weight_grad)
    w_out.start()
    lo_out.wait()
    ng_out.wait()
    w_out.wait()
    for ex in done:
        ex.drain()
    for p in range(Y):
        hub_to.copy(p).wait_send()
        core_to.copy(p).wait_send()
    gx.each(lambda peer: w_to.copy(peer).wait_send())


def yc_row(c, Y, y):
    return c * Y + y


def from_peer_major(dims):
    Y, Z, C, CUT = dims[0], dims[1], dims[2], dims[9]
    DOM = Y * Z * C

    def source(i):
        k, q = div_(i, DOM), mod_(i, DOM)
        cc, zz, yy = mod_(q, C), mod_(div_(q, C), Z), div_(q, C * Z)
        return ((yy * C + cc) * Z + zz) * CUT + k

    return source


def copy_kernel(*refs):
    n = len(refs) // 2
    for src, dst in zip(refs[:n], refs[n:]):
        dst[...] = src[...]


def per_device(
    sizes,
    node_feats,
    neigh_weight,
    bias,
    out_grad,
    tile_values,
    tile_src,
    tile_dst,
    tile_count,
    hub_rows,
    send_rows,
):
    Y, Z, C, X = sizes
    N, F = node_feats.shape
    NT, T = tile_values.shape[:2]
    CUT = send_rows.shape[1]
    HD = hub_rows.shape[0]
    DOM = Y * Z * C
    HALO = DOM * CUT
    NB, SB = N // T, (N + HALO + DOM * HD) // T
    D, R = X * F, N // X
    ZC, YCC = Z * CUT, Y * C * CUT
    DY = D // Y
    DZ = DY // Z

    at = jnp.arange(NT, dtype=jnp.int32)
    key = jnp.where(at < tile_count[0], tile_dst * SB + tile_src, -1)
    same = (key[:, None] == key[None, :]) & (at[None, :] < at[:, None])
    prev = jnp.max(jnp.where(same, at[None, :] + 1, 0), axis=1)
    place = jnp.arange(NB * SB, dtype=jnp.int32)
    last = jnp.max(jnp.where(place[:, None] == key[None, :], at[None, :] + 1, 0), axis=1)

    dims = (Y, Z, C, X, N, T, NT, F, HD, CUT, 1.0 / math.sqrt(N * DOM))
    vm = pl.BlockSpec(memory_space=pltpu.VMEM)
    sm = pl.BlockSpec(memory_space=pltpu.SMEM)
    hbm = pl.BlockSpec(memory_space=pl.ANY)

    def b(*shape):
        return pltpu.VMEM(shape, BF16)

    def f(*shape):
        return pltpu.VMEM(shape, F32)

    def sem(n):
        return pltpu.SemaphoreType.DMA((2, n))

    inputs = dict(
        node_feats=(node_feats, hbm),
        weight=(neigh_weight, hbm),
        out_grad=(out_grad, hbm),
        tiles=(tile_values, hbm),
        bias=(bias[None, :], vm),
        sends=(send_rows.T, vm),
        hub_ids=(hub_rows[None, :], vm),
        prev=(prev, sm),
        last=(last, sm),
    )
    outputs = dict(
        layer_out=(jax.ShapeDtypeStruct((X, R, F), BF16), hbm),
        node_grad=(jax.ShapeDtypeStruct((N, F), BF16), hbm),
        weight_grad=(jax.ShapeDtypeStruct((C * Y, Z, DZ, F), F32), hbm),
        bias_grad=(jax.ShapeDtypeStruct((1, F), F32), vm),
    )
    scratch = dict(
        nf=b(N, F),
        tile_buf=b(NT, T, T),
        turned=b(NT, T, T),
        acc_tiles_t=b(NT + 1, T, T),
        adj_t=b(SB * T, N),
        hot=b(HALO, N),
        hot_t=b(N, HALO),
        out_halo=b(Y * C, ZC, F),
        st1=b(Y * C, ZC, F),
        st2=b(Z, YCC, F),
        halo_z=b(Z, YCC, F),
        hub=b(Y, Z, C, HD, F),
        acc=f(F + 16, N),
        inv=f(8, N),
        selfc=b(R, D),
        meanc=b(R, D),
        ogc=b(R, D),
        wfull=b(2 * D, D),
        bias8=f(8, F),
        biasc=f(8, D),
        mean=b(N, F),
        pre=f(R, D),
        lo_send=b(R, D),
        lo_recv=b(X, R, F),
        wv=b(2 * D, F),
        ogv=b(N, F),
        wg_all=f(C * Y, Z, DZ, F),
        wb_all=b(C * Y, DY, F),
        gp=b(R, D),
        gm_send=b(X, R, F),
        gm=b(X, R, F),
        gs_send=b(X, R, F),
        gs_recv=b(X, R, F),
        wg32=f(C, D, D),
        wgb=b(C, D, D),
        wg_core=b(C, D, D),
        wx_send=b(X, D + 16, F),
        wx_recv=b(X, D + 16, F),
        wx_own=f(X, D + 8, F),
        wy_send=b(Y, DY + 16, F),
        wy_recv=b(Y, DY + 16, F),
        wy_own=f(Y, DY, F),
        wz_send=f(Z, DZ + 8, F),
        wz_recv=f(Z, DZ + 8, F),
        wout=f(Z, DZ, F),
        bias_core=f(C, 8, F),
        hs32=f(C, Y, Z, HD, F),
        hsb=b(C, Y, Z, HD, F),
        hs_core=b(Y, Z, HD, F),
        hy_send=b(Y, Z, HD, F),
        hy_recv=b(Y, Z, HD, F),
        hy_own=f(Z, HD, F),
        hz_send=b(Z, HD, F),
        hz_recv=b(Z, HD, F),
        halo_zb=b(Z, YCC, F),
        rt1=b(Z, YCC, F),
        halo_m=b(Y * C, ZC, F),
        rt2=b(Y * C, ZC, F),
        total=f(N, F),
        ng=b(N, F),
        local_sem=pltpu.SemaphoreType.DMA((8,)),
        s_yc=sem(Y * C),
        s_z=sem(Z),
        s_hz=sem(Z),
        s_hy=sem(Y),
        s_hc=sem(Y),
        s_xs=sem(X),
        s_xo=sem(X),
        s_xw=sem(X),
        s_xb=sem(X),
        s_wc=sem(X),
        s_xm=sem(X),
        s_xl=sem(X),
        s_xg=sem(X),
        s_xgs=sem(X),
        s_gc=sem(C),
        s_gx=sem(X),
        s_gy=sem(Y),
        s_gz=sem(Z),
        s_az=sem(Z),
        s_ay=sem(Y * C),
        s_bc=sem(C),
        s_bhc=sem(Y),
        s_bhy=sem(Y),
        s_bhz=sem(Z),
        s_rz=sem(Z),
        s_ryc=sem(Y * C),
    )
    names = list(inputs) + list(outputs) + list(scratch)
    results = pl.pallas_call(
        functools.partial(kernel, dims, names),
        out_shape=[shape for shape, _ in outputs.values()],
        in_specs=[spec for _, spec in inputs.values()],
        out_specs=[spec for _, spec in outputs.values()],
        scratch_shapes=list(scratch.values()),
        compiler_params=pltpu.CompilerParams(
            collective_id=0, has_side_effects=True, vmem_limit_bytes=60 * 1024 * 1024
        ),
    )(*[array for array, _ in inputs.values()])
    layer_out, node_grad, weight_grad, bias_grad = pl.pallas_call(
        copy_kernel,
        out_shape=[jax.ShapeDtypeStruct(v.shape, v.dtype) for v in results],
        in_specs=[vm] * 4,
        out_specs=[vm] * 4,
    )(*results)
    return (
        layer_out.reshape(N, F),
        node_grad,
        weight_grad.reshape(2 * D, F),
        bias_grad.reshape(F),
    )


def solution(mesh, y_chips=Y_CHIPS):
    dom, feat = mesh.shape["dom"], mesh.shape["feat"]
    sizes = (y_chips, dom // (CORES * y_chips), CORES, feat)
    in_specs = (
        P("dom", "feat"),
        P(None, "feat"),
        P("feat"),
        P("dom", "feat"),
        P("dom", None, None),
        P("dom"),
        P("dom"),
        P("dom"),
        P("dom"),
        P("dom", None),
    )
    out_specs = (P("dom", "feat"), P("dom", "feat"), P(None, "feat"), P("feat"))
    return jax.shard_map(
        functools.partial(per_device, sizes),
        mesh=mesh,
        in_specs=in_specs,
        out_specs=out_specs,
        check_vma=False,
    )
```

```python
import functools
import math
import types

import jax
import jax.numpy as jnp
from jax import lax
from jax.experimental import pallas as pl
from jax.experimental.pallas import tpu as pltpu
from jax.sharding import PartitionSpec as P

BF16 = jnp.bfloat16
F32 = jnp.float32
CORES = 2
Y_CHIPS = 4


def dot(a, b):
    return jnp.dot(a, b, preferred_element_type=F32)


def dot_nt(a, b):
    return lax.dot_general(a, b, (((1,), (1,)), ((), ())), preferred_element_type=F32)


def dot_tn(a, b):
    return lax.dot_general(a, b, (((0,), (0,)), ((), ())), preferred_element_type=F32)


class Group:
    def __init__(self, size, me, device):
        self.size, self.me, self.device = size, me, device

    def each(self, body):
        for step in range(1, self.size):
            body((self.me + step) & (self.size - 1))


class Exchange:
    def __init__(self, group, src, dst, sems, sent, landed, each=False):
        self.group, self.src, self.dst, self.sems = group, src, dst, sems
        self.sent, self.landed, self.one_by_one = sent, landed, each

    def copy(self, peer, landing):
        return pltpu.make_async_remote_copy(
            src_ref=self.src(peer),
            dst_ref=self.dst(landing),
            send_sem=self.sems.at[0, 0],
            recv_sem=self.sems.at[1, landing if self.one_by_one else 0],
            device_id=self.group.device(peer),
            device_id_type=pl.DeviceIdType.MESH,
        )

    def all(self, part):
        return pltpu.make_async_remote_copy(
            src_ref=part,
            dst_ref=part,
            send_sem=self.sems.at[0, 0],
            recv_sem=self.sems.at[1, 0],
            device_id=self.group.device((self.group.me + 1) & (self.group.size - 1)),
            device_id_type=pl.DeviceIdType.MESH,
        )

    def start_to(self, peer):
        self.copy(peer, self.group.me).start()

    def start(self):
        self.group.each(self.start_to)

    def wait(self):
        if self.group.size == 1:
            return
        self.all(self.landed).wait_recv()

    def wait_then(self, after):
        def body(peer):
            self.copy(peer, peer).wait_recv()
            after(peer)

        self.group.each(body)

    def drain(self):
        if self.group.size == 1:
            return
        self.all(self.sent).wait_send()


class Relay:
    def __init__(self, device, sems, src, dst):
        self.device, self.sems, self.src, self.dst = device, sems, src, dst

    def copy(self, slot):
        return pltpu.make_async_remote_copy(
            src_ref=self.src(slot),
            dst_ref=self.dst(slot),
            send_sem=self.sems.at[0, slot],
            recv_sem=self.sems.at[1, slot],
            device_id=self.device,
            device_id_type=pl.DeviceIdType.MESH,
        )

    def start(self, slot):
        self.copy(slot).start()


def log2(n):
    return n.bit_length() - 1


def div_(a, n):
    return lax.shift_right_logical(a, log2(n))


def mod_(a, n):
    return a & (n - 1)


def aligned(start, size):
    return pl.ds(pl.multiple_of(start, size), size)


def kernel(dims, names, *refs):
    r = types.SimpleNamespace(**dict(zip(names, refs)))
    Y, Z, C, X, N, T, NT, F, HD, CUT, scale = dims
    D = X * F
    R = N // X
    DOM = Y * Z * C
    HALO = DOM * CUT
    NB = N // T
    SB = (N + HALO + DOM * HD) // T
    ZC, YCC = Z * CUT, Y * C * CUT
    PERY = Z * C * HD
    DY = D // Y
    RES = Z // 4 if Z >= 8 else Z
    ZQ = Z // RES
    DN = DY // RES
    dom, x = lax.axis_index("dom"), lax.axis_index("feat")
    c = dom & (C - 1)
    z = (dom >> log2(C)) & (Z - 1)
    y = dom >> log2(C * Z)
    yc = y * C + c

    def at(yy, zz, cc):
        return ((yy * Z + zz) * C + cc, x)

    gyc = Group(Y * C, yc, lambda p: at(p >> log2(C), z, p & (C - 1)))
    gz = Group(Z, z, lambda p: at(y, p, c))
    gy = Group(Y, y, lambda p: at(p, z, c))
    zr, zq = z & (RES - 1), z >> log2(RES)

    def near(p):
        step = (p - zr) & (RES - 1)
        step = jnp.where(step > RES // 2, step - RES, step)
        return at(y, (z + step) & (Z - 1), c)

    gfar = Group(Z // RES, zq, lambda p: at(y, (p << log2(RES)) | zr, c))
    gnear = Group(RES, zr, near)
    gc = Group(C, c, lambda p: at(y, z, p))
    gx = Group(X, x, lambda p: (dom, p))
    other_core = at(y, z, 1 - c)

    barrier = pltpu.get_barrier_semaphore()
    for group in (gyc, gz, gx):
        group.each(
            lambda peer, group=group: pl.semaphore_signal(
                barrier, inc=1, device_id=group.device(peer), device_id_type=pl.DeviceIdType.MESH
            )
        )

    def rows_of(p):
        return aligned(p * R, R)

    def cols_of(p):
        return aligned(p * F, F)

    def local(i, src, dst):
        return pltpu.make_async_copy(src, dst, r.local_sem.at[i])

    fetch_nf = local(0, r.node_feats, r.nf)
    fetch_tiles = local(1, r.tiles, r.tile_buf)
    fetch_w = local(2, r.weight, r.wv)
    fetch_og = local(3, r.out_grad, r.ogv)
    fetch_nf.start()
    fetch_w.start()
    fetch_og.start()
    fetch_tiles.start()

    eye = lax.broadcasted_iota(jnp.int32, (DOM, DOM), 0) == lax.broadcasted_iota(
        jnp.int32, (DOM, DOM), 1
    )
    for k in range(CUT):
        wide = jnp.broadcast_to(r.sends[k : k + 1, :], (DOM, DOM)).astype(F32)
        col = jnp.sum(jnp.where(eye, wide, 0.0), axis=1, keepdims=True).astype(jnp.int32)
        r.hot[k * DOM : (k + 1) * DOM, :] = (
            col == lax.broadcasted_iota(jnp.int32, (DOM, N), 1)
        ).astype(BF16)
    eye = lax.broadcasted_iota(jnp.int32, (HD, HD), 0) == lax.broadcasted_iota(
        jnp.int32, (HD, HD), 1
    )
    wide = jnp.broadcast_to(r.hub_ids[...], (HD, HD)).astype(F32)
    col = jnp.sum(jnp.where(eye, wide, 0.0), axis=1, keepdims=True).astype(jnp.int32)
    hub_hot = (col == lax.broadcasted_iota(jnp.int32, (HD, N), 1)).astype(BF16)

    def perm(source_of):
        row = lax.broadcasted_iota(jnp.int32, (HALO, HALO), 0)
        lane = lax.broadcasted_iota(jnp.int32, (HALO, HALO), 1)
        return (source_of(row) == lane).astype(BF16)

    def peer_major(i):
        k, zz = mod_(i, CUT), mod_(div_(i, CUT), Z)
        cc, yy = mod_(div_(i, ZC), C), div_(i, ZC * C)
        return k * DOM + (yy * Z + zz) * C + cc

    def z_major(i):
        return (mod_(div_(i, CUT), Y * C) * Z + div_(i, YCC)) * CUT + mod_(i, CUT)

    def yc_major(i):
        return (mod_(div_(i, CUT), Z) * (Y * C) + div_(i, ZC)) * CUT + mod_(i, CUT)

    def to_dom(i):
        yy = div_(i, Z * C * CUT)
        zz = mod_(div_(i, C * CUT), Z)
        return (zz * Y + yy) * (C * CUT) + mod_(i, C * CUT)

    def from_dom(i):
        zz = div_(i, Y * C * CUT)
        yy = mod_(div_(i, C * CUT), Y)
        return (yy * Z + zz) * (C * CUT) + mod_(i, C * CUT)

    fetch_nf.wait()
    r.hub[y, zq, zr, c] = dot(hub_hot, r.nf[...]).astype(BF16)
    picked = dot(r.hot[...], r.nf[...]).astype(BF16)
    r.out_halo[...] = dot(perm(peer_major), picked).astype(BF16).reshape(Y * C, ZC, F)
    r.bias8[...] = jnp.broadcast_to(r.bias[...], (8, F))
    pl.semaphore_wait(barrier, Y * C + Z + X - 3)

    done = []

    def most(ref):
        return ref.at[pl.ds(0, ref.shape[0] - 1)]

    def cols3(ref):
        return ref.at[:, 0 : D - F]


    def exchange(group, src, dst, sems, sent, landed, each=False):
        ex = Exchange(group, src, dst, sems, sent, landed, each)
        done.append(ex)
        return ex

    ex_yc = exchange(
        gyc, lambda p: r.out_halo.at[p], lambda p: r.st1.at[p],
        r.s_yc,
        most(r.out_halo),
        most(r.st1),
    )
    ex_yc.start()
    ex_hz = exchange(
        gfar,
        lambda p: r.hub.at[y, zq, zr, c],
        lambda p: r.hub.at[y, p, zr, c],
        r.s_hz,
        r.hub.at[y, pl.ds(0, ZQ - 1), zr, c],
        r.hub.at[y, pl.ds(0, ZQ - 1), zr, c],
    )
    ex_hz.start()
    r.st1[yc] = r.out_halo[yc]

    wrows = aligned(c * D, D)
    fetch_w.wait()
    fetch_og.wait()
    ex_xw = exchange(
        gx, lambda p: r.wv.at[wrows], lambda p: r.wfull.at[wrows, cols_of(p)],
        r.s_xw,
        r.wfull.at[wrows, 0 : D - F],
        r.wfull.at[wrows, 0 : D - F],
        each=True,
    )
    ex_xw.start()
    ex_xs = exchange(
        gx, lambda p: r.nf.at[rows_of(p)], lambda p: r.selfc.at[:, cols_of(p)],
        r.s_xs,
        cols3(r.selfc),
        cols3(r.selfc),
    )
    ex_xs.start()
    ex_xb = exchange(
        gx, lambda p: r.bias8, lambda p: r.biasc.at[:, cols_of(p)],
        r.s_xb,
        cols3(r.biasc),
        cols3(r.biasc),
    )
    ex_xb.start()
    ex_xo = exchange(
        gx, lambda p: r.ogv.at[rows_of(p)], lambda p: r.ogc.at[:, cols_of(p)],
        r.s_xo,
        cols3(r.ogc),
        cols3(r.ogc),
    )
    ex_xo.start()
    r.biasc[:, cols_of(x)] = r.bias8[...]
    r.selfc[:, cols_of(x)] = r.nf[rows_of(x), :]
    r.ogc[:, cols_of(x)] = r.ogv[rows_of(x), :]
    r.wfull[:, cols_of(x)] = r.wv[...]

    fetch_tiles.wait()
    turn = NT // 8 if NT % 8 == 0 else 1

    def turn_tiles(i, carry):
        for k in range(NT // turn):
            t = i * (NT // turn) + k
            r.turned[t] = r.tile_buf[t].T
        return carry

    lax.fori_loop(0, turn, turn_tiles, 0)
    r.acc_tiles_t[0] = jnp.zeros((T, T), BF16)

    ex_hz.wait()
    ex_hn = exchange(
        gnear,
        lambda p: r.hub.at[y, :, zr, c],
        lambda p: r.hub.at[y, :, p, c],
        r.s_hn,
        r.hub.at[y, :, pl.ds(0, RES - 1), c],
        r.hub.at[y, :, pl.ds(0, RES - 1), c],
    )
    ex_hn.start()

    def add_tile(t, carry):
        r.acc_tiles_t[t + 1] = r.turned[t] + r.acc_tiles_t[r.prev[t]]
        return carry

    lax.fori_loop(0, NT, add_tile, 0)

    ex_yc.wait()
    r.halo_z[...] = (
        dot(perm(z_major), r.st1[...].reshape(HALO, F)).astype(BF16).reshape(Z, YCC, F)
    )
    ex_z = exchange(
        gz, lambda p: r.halo_z.at[p], lambda p: r.st2.at[p],
        r.s_z,
        most(r.halo_z),
        most(r.st2),
    )
    ex_z.start()
    r.st2[z] = r.halo_z[z]

    ex_hn.wait()
    ex_hy = exchange(
        gy, lambda p: r.hub.at[y, :, :, c], lambda p: r.hub.at[p, :, :, c],
        r.s_hy,
        r.hub.at[pl.ds(0, Y - 1), :, :, c],
        r.hub.at[pl.ds(0, Y - 1), :, :, c],
        each=True,
    )
    ex_hy.start()
    hub_to = Relay(other_core, r.s_hc, lambda p: r.hub.at[p, :, :, c], lambda p: r.hub.at[p, :, :, c])
    hub_from = Relay(
        other_core, r.s_hc, lambda p: r.hub.at[p, :, :, 1 - c], lambda p: r.hub.at[p, :, :, 1 - c]
    )
    hub_to.start(y)

    w_to = Relay(
        other_core,
        r.s_wc,
        lambda p: r.wfull.at[wrows, cols_of(p)],
        lambda p: r.wfull.at[wrows, cols_of(p)],
    )
    other_rows = aligned((1 - c) * D, D)
    w_from = Relay(
        other_core,
        r.s_wc,
        lambda p: r.wfull.at[other_rows, cols_of(p)],
        lambda p: r.wfull.at[other_rows, cols_of(p)],
    )
    def place(s, carry):
        for n in range(NB):
            r.adj_t[aligned(s * T, T), n * T : (n + 1) * T] = r.acc_tiles_t[r.last[n * SB + s]]
        return carry

    lax.fori_loop(0, SB, place, 0)

    def gather(rows, source):
        ones = jnp.ones((16, source.shape[0]), BF16)
        return dot(jnp.concatenate([source.T, ones], axis=0), r.adj_t[rows, :])

    def add_hub(p):
        rows = pl.ds(pl.multiple_of(N + HALO + p * PERY, T), PERY)
        r.acc[...] += gather(rows, r.hub[p].reshape(PERY, F))

    r.acc[...] = gather(slice(0, N), r.nf[...])
    hub_from.copy(y).wait_recv()
    add_hub(y)

    ex_xw.wait_then(w_to.start)
    ex_hy.wait_then(hub_to.start)

    ex_z.wait()
    halo = dot(perm(to_dom), r.st2[...].reshape(HALO, F)).astype(BF16)
    r.acc[...] += gather(slice(N, N + HALO), halo)

    for i in range(1, Y):
        p = (y + i) & (Y - 1)
        hub_from.copy(p).wait_recv()
        add_hub(p)
    r.inv[...] = 1.0 / jnp.maximum(r.acc[F : F + 8, :], 1.0)
    r.mean[...] = (r.acc[0:F, :] * r.inv[0:1, :]).astype(BF16).T
    ex_xm = exchange(
        gx, lambda p: r.mean.at[rows_of(p)], lambda p: r.meanc.at[:, cols_of(p)],
        r.s_xm,
        cols3(r.meanc),
        cols3(r.meanc),
    )
    ex_xm.start()
    r.meanc[:, cols_of(x)] = r.mean[rows_of(x), :]

    ex_xs.wait()
    ex_xb.wait()
    ex_xo.wait()
    gx.each(lambda peer: w_from.copy(peer).wait_recv())
    r.pre[...] = dot(r.selfc[...], r.wfull[0:D, :]) + r.biasc[0:1, :]

    for k in range(CUT):
        row = jnp.broadcast_to(r.sends[k : k + 1, :], (N, DOM))
        r.hot_t[:, k * DOM : (k + 1) * DOM] = (
            row == lax.broadcasted_iota(jnp.int32, (N, DOM), 0)
        ).astype(BF16)

    inv_rows = jnp.broadcast_to(r.inv[0:1, rows_of(x)], (F, R)).T
    ex_xm.wait()
    pre_act = r.pre[...] + dot(r.meanc[...], r.wfull[D : 2 * D, :])
    sig = jax.nn.sigmoid(pre_act)
    r.gp[...] = (r.ogc[...].astype(F32) * (sig * (1.0 + pre_act * (1.0 - sig)))).astype(BF16)
    r.lo_send[...] = (pre_act * sig).astype(BF16)
    cat_mean = dot_nt(r.gp[...], r.wfull[D : 2 * D, :])
    for j in range(X):
        r.gm_send[j] = (cat_mean[:, j * F : (j + 1) * F] * inv_rows).astype(BF16)
    ex_xg = exchange(
        gx, lambda p: r.gm_send.at[p], lambda p: r.gm.at[p],
        r.s_xg,
        most(r.gm_send),
        most(r.gm),
    )
    ex_xg.start()
    r.gm[x] = r.gm_send[x]

    for half, src in enumerate((r.selfc, r.meanc)):
        for q in range(0, D, 2 * T):
            part = dot_tn(src[:, q : q + 2 * T], r.gp[...])
            r.wg32[half, q : q + 2 * T, :] = part
            r.wgb[half, q : q + 2 * T, :] = part.astype(BF16)
    ex_gc = exchange(
        gc, lambda p: r.wgb.at[p], lambda p: r.wg_core.at[p],
        r.s_gc,
        most(r.wgb),
        most(r.wg_core),
    )
    ex_gc.start()
    bias_sum = jnp.sum(r.gp[...].astype(F32), axis=0, keepdims=True)

    def bias_rows(value):
        full = jnp.broadcast_to(value, (8, F))
        high = full.astype(BF16).astype(F32)
        return jnp.concatenate([high, full - high], axis=0).astype(BF16)

    def bias_of(rows):
        wide = rows.astype(F32)
        return wide[0:8] + wide[8:16]

    cat_self = dot_nt(r.gp[...], r.wfull[0:D, :])
    for j in range(X):
        r.gs_send[j] = cat_self[:, j * F : (j + 1) * F].astype(BF16)
    ex_gc.wait()
    for j in range(X):
        cols = slice(j * F, (j + 1) * F)
        block = r.wg32[c, :, cols] + r.wg_core[1 - c, :, cols].astype(F32)
        r.wx_own[j, 0:D, :] = block
        r.wx_send[j, 0:D, :] = block.astype(BF16)
        r.wx_own[j, D : D + 8, :] = jnp.broadcast_to(bias_sum[:, cols], (8, F))
        r.wx_send[j, D : D + 16, :] = bias_rows(bias_sum[:, cols])
    ex_gx = exchange(
        gx, lambda p: r.wx_send.at[p], lambda p: r.wx_recv.at[p],
        r.s_gx,
        most(r.wx_send),
        most(r.wx_recv),
    )
    ex_gx.start()

    ex_xg.wait()
    core_to = Relay(
        other_core, r.s_bhc, lambda p: r.hsb.at[1 - c, p], lambda p: r.hs_core.at[p]
    )
    ex_bhy = exchange(
        gy, lambda p: r.hy_send.at[p], lambda p: r.hy_recv.at[p],
        r.s_bhy,
        most(r.hy_send),
        most(r.hy_recv),
    )

    def spread(rows):
        return dot(r.adj_t[rows, :], r.gm[...].reshape(N, F))

    def back_hub(p):
        rows = spread(pl.ds(pl.multiple_of(N + HALO + p * PERY, T), PERY)).reshape(Z, C, HD, F)
        for cc in range(C):
            r.hs32[cc, p] = rows[:, cc]
            r.hsb[cc, p] = rows[:, cc].astype(BF16)
        core_to.start(p)

    def pair_hub(p, own):
        core_to.copy(p).wait_recv()
        pair = r.hs32[c, p] + r.hs_core[p].astype(F32)
        if own:
            r.hy_own[...] = pair
        else:
            r.hy_send[p] = pair.astype(BF16)
            ex_bhy.start_to(p)

    order = [(y + i) & (Y - 1) for i in range(1, Y)] + [y]
    back_hub(order[0])
    for i in range(1, Y):
        back_hub(order[i])
        pair_hub(order[i - 1], False)

    halo_b = spread(slice(N, N + HALO)).astype(BF16)
    r.halo_zb[...] = dot(perm(from_dom), halo_b).astype(BF16).reshape(Z, YCC, F)
    ex_rz = exchange(
        gz, lambda p: r.halo_zb.at[p], lambda p: r.rt1.at[p],
        r.s_rz,
        most(r.halo_zb),
        most(r.rt1),
    )
    ex_rz.start()
    r.rt1[z] = r.halo_zb[z]

    pair_hub(y, True)

    r.wx_recv[x] = jnp.zeros((D + 16, F), BF16)
    ex_gx.wait()
    wsum = r.wx_own[x, 0:D, :]
    bsum = r.wx_own[x, D : D + 8, :]
    for j in range(X):
        wsum = wsum + r.wx_recv[j, 0:D, :].astype(F32)
        bsum = bsum + bias_of(r.wx_recv[j, D : D + 16, :])
    for j in range(Y):
        block = wsum[j * DY : (j + 1) * DY]
        r.wy_own[j] = block
        r.wy_send[j, 0:DY, :] = block.astype(BF16)
        r.wy_send[j, DY : DY + 16, :] = bias_rows(bsum[0:1])
    ex_gy = exchange(
        gy, lambda p: r.wy_send.at[p], lambda p: r.wy_recv.at[p],
        r.s_gy,
        most(r.wy_send),
        most(r.wy_recv),
    )
    ex_gy.start()

    ex_xgs = exchange(
        gx, lambda p: r.gs_send.at[p], lambda p: r.gs_recv.at[p],
        r.s_xgs,
        most(r.gs_send),
        most(r.gs_recv),
    )
    ex_xgs.start()
    ex_xl = exchange(
        gx, lambda p: r.lo_send.at[:, cols_of(p)], lambda p: r.lo_recv.at[p],
        r.s_xl,
        cols3(r.lo_send),
        most(r.lo_recv),
    )
    ex_xl.start()
    r.lo_recv[x] = r.lo_send[:, cols_of(x)]
    r.gs_recv[x] = r.gs_send[x]

    r.total[...] = spread(slice(0, N))

    r.wy_recv[y] = jnp.zeros((DY + 16, F), BF16)
    ex_gy.wait()
    wsum = r.wy_own[y]
    for j in range(Y):
        wsum = wsum + r.wy_recv[j, 0:DY, :].astype(F32)
        bsum = bsum + bias_of(r.wy_recv[j, DY : DY + 16, :])
    for p in range(RES):
        block = wsum[p * DN : (p + 1) * DN]
        r.wn_own[p] = block
        r.wn_send[p, 0:DN, :] = block.astype(BF16)
        r.wn_send[p, DN : DN + 16, :] = bias_rows(bsum[0:1])
    ex_gn = exchange(
        gnear,
        lambda p: r.wn_send.at[p],
        lambda p: r.wn_recv.at[p],
        r.s_gn,
        most(r.wn_send),
        most(r.wn_recv),
    )
    ex_gn.start()

    r.hy_recv[y] = jnp.zeros((Z, HD, F), BF16)
    ex_bhy.wait()
    hub_y = r.hy_own[...]
    for p in range(Y):
        hub_y = hub_y + r.hy_recv[p].astype(F32)
    hub_y = hub_y.reshape(ZQ, RES, HD, F)
    for p in range(RES):
        r.hz_own[p] = hub_y[:, p]
        r.hz_send[p] = hub_y[:, p].astype(BF16)
    ex_bhn = exchange(
        gnear,
        lambda p: r.hz_send.at[p],
        lambda p: r.hz_recv.at[p],
        r.s_bhn,
        most(r.hz_send),
        most(r.hz_recv),
    )
    ex_bhn.start()

    r.wn_recv[zr] = jnp.zeros((DN + 16, F), BF16)
    ex_gn.wait()
    wsum = r.wn_own[zr]
    for p in range(RES):
        wsum = wsum + r.wn_recv[p, 0:DN, :].astype(F32)
        bsum = bsum + bias_of(r.wn_recv[p, DN : DN + 16, :])
    r.wf_all[zq, 0:DN, :] = wsum.astype(BF16)
    r.wf_all[zq, DN : DN + 16, :] = bias_rows(bsum[0:1])
    ex_gf = exchange(
        gfar,
        lambda p: r.wf_all.at[zq],
        lambda p: r.wf_all.at[p],
        r.s_gf,
        most(r.wf_all),
        most(r.wf_all),
    )
    ex_gf.start()

    ex_rz.wait()
    r.halo_m[...] = (
        dot(perm(yc_major), r.rt1[...].reshape(HALO, F)).astype(BF16).reshape(Y * C, ZC, F)
    )
    ex_ryc = exchange(
        gyc, lambda p: r.halo_m.at[p], lambda p: r.rt2.at[p],
        r.s_ryc,
        most(r.halo_m),
        most(r.rt2),
    )
    ex_ryc.start()
    r.rt2[yc] = r.halo_m[yc]

    r.hz_recv[zr] = jnp.zeros((ZQ, HD, F), BF16)
    ex_bhn.wait()
    hub_z = r.hz_own[zr] + jnp.sum(r.hz_recv[...].astype(F32), axis=0)
    r.hf_own[...] = hub_z
    r.hf_send[...] = hub_z.astype(BF16)
    ex_bhf = exchange(
        gfar,
        lambda p: r.hf_send.at[p],
        lambda p: r.hf_recv.at[p],
        r.s_bhf,
        most(r.hf_send),
        most(r.hf_recv),
    )
    ex_bhf.start()

    ex_gf.wait()
    for q in range(ZQ):
        far = r.wf_all[q].astype(F32)
        wtotal = far[0:DN] if q == 0 else wtotal + far[0:DN]
        btotal = bias_of(far[DN : DN + 16]) + (0.0 if q == 0 else btotal)
    r.wa[zr] = (wtotal * scale).astype(BF16)
    r.bias_core[c] = btotal * scale
    ex_az = exchange(
        gnear, lambda p: r.wa.at[zr], lambda p: r.wa.at[p], r.s_az, most(r.wa), most(r.wa)
    )
    ex_az.start()
    ex_bc = exchange(
        gc, lambda p: r.bias_core.at[c], lambda p: r.bias_core.at[p],
        r.s_bc,
        most(r.bias_core),
        most(r.bias_core),
    )
    ex_bc.start()

    ex_xgs.wait()
    for j in range(X):
        r.total[j * R : (j + 1) * R, :] += r.gs_recv[j].astype(F32)

    ex_ryc.wait()
    returned = dot(perm(from_peer_major(dims)), r.rt2[...].reshape(HALO, F)).astype(BF16)
    r.total[...] += dot(r.hot_t[...], returned)

    ex_az.wait()
    r.wb_all[yc_row(c, Y, y)] = r.wa[...].reshape(DY, F)
    ex_ay = exchange(
        gyc,
        lambda p: r.wb_all.at[yc_row(c, Y, y)],
        lambda p: r.wb_all.at[yc_row(p & (C - 1), Y, p >> log2(C))],
        r.s_ay,
        most(r.wb_all),
        most(r.wb_all),
    )
    ex_ay.start()

    r.hf_recv[zq] = jnp.zeros((HD, F), BF16)
    ex_bhf.wait()
    hub_mine = r.hf_own[zq] + jnp.sum(r.hf_recv[...].astype(F32), axis=0)
    high = hub_mine.astype(BF16)
    low = (hub_mine - high.astype(F32)).astype(BF16)
    hub_hot_t = (
        jnp.broadcast_to(r.hub_ids[...], (N, HD)) == lax.broadcasted_iota(jnp.int32, (N, HD), 0)
    ).astype(BF16)
    r.ng[...] = (r.total[...] + dot(hub_hot_t, high) + dot(hub_hot_t, low)).astype(BF16)
    ng_out = local(6, r.ng, r.node_grad)
    ng_out.start()


    ex_xl.wait()
    lo_out = local(5, r.lo_recv, r.layer_out)
    lo_out.start()

    ex_bc.wait()
    r.bias_grad[...] = r.bias_core[0, 0:1] + r.bias_core[1, 0:1]
    ex_ay.wait()
    r.wg_all[...] = r.wb_all[...].astype(F32)

    w_out = local(7, r.wg_all, r.weight_grad)
    w_out.start()
    lo_out.wait()
    ng_out.wait()
    w_out.wait()
    for ex in done:
        ex.drain()
    for p in range(Y):
        hub_to.copy(p).wait_send()
        core_to.copy(p).wait_send()
    gx.each(lambda peer: w_to.copy(peer).wait_send())


def yc_row(c, Y, y):
    return c * Y + y


def from_peer_major(dims):
    Y, Z, C, CUT = dims[0], dims[1], dims[2], dims[9]
    DOM = Y * Z * C

    def source(i):
        k, q = div_(i, DOM), mod_(i, DOM)
        cc, zz, yy = mod_(q, C), mod_(div_(q, C), Z), div_(q, C * Z)
        return ((yy * C + cc) * Z + zz) * CUT + k

    return source


def copy_kernel(*refs):
    n = len(refs) // 2
    for src, dst in zip(refs[:n], refs[n:]):
        dst[...] = src[...]


def per_device(
    sizes,
    node_feats,
    neigh_weight,
    bias,
    out_grad,
    tile_values,
    tile_src,
    tile_dst,
    tile_count,
    hub_rows,
    send_rows,
):
    Y, Z, C, X = sizes
    N, F = node_feats.shape
    NT, T = tile_values.shape[:2]
    CUT = send_rows.shape[1]
    HD = hub_rows.shape[0]
    DOM = Y * Z * C
    HALO = DOM * CUT
    NB, SB = N // T, (N + HALO + DOM * HD) // T
    D, R = X * F, N // X
    ZC, YCC = Z * CUT, Y * C * CUT
    DY = D // Y
    RES = Z // 4 if Z >= 8 else Z
    ZQ = Z // RES
    DN = DY // RES

    at = jnp.arange(NT, dtype=jnp.int32)
    key = jnp.where(at < tile_count[0], tile_dst * SB + tile_src, -1)
    same = (key[:, None] == key[None, :]) & (at[None, :] < at[:, None])
    prev = jnp.max(jnp.where(same, at[None, :] + 1, 0), axis=1)
    place = jnp.arange(NB * SB, dtype=jnp.int32)
    last = jnp.max(jnp.where(place[:, None] == key[None, :], at[None, :] + 1, 0), axis=1)

    dims = (Y, Z, C, X, N, T, NT, F, HD, CUT, 1.0 / math.sqrt(N * DOM))
    vm = pl.BlockSpec(memory_space=pltpu.VMEM)
    sm = pl.BlockSpec(memory_space=pltpu.SMEM)
    hbm = pl.BlockSpec(memory_space=pl.ANY)

    def b(*shape):
        return pltpu.VMEM(shape, BF16)

    def f(*shape):
        return pltpu.VMEM(shape, F32)

    def sem(n):
        return pltpu.SemaphoreType.DMA((2, n))

    inputs = dict(
        node_feats=(node_feats, hbm),
        weight=(neigh_weight, hbm),
        out_grad=(out_grad, hbm),
        tiles=(tile_values, hbm),
        bias=(bias[None, :], vm),
        sends=(send_rows.T, vm),
        hub_ids=(hub_rows[None, :], vm),
        prev=(prev, sm),
        last=(last, sm),
    )
    outputs = dict(
        layer_out=(jax.ShapeDtypeStruct((X, R, F), BF16), hbm),
        node_grad=(jax.ShapeDtypeStruct((N, F), BF16), hbm),
        weight_grad=(jax.ShapeDtypeStruct((C * Y, DY, F), F32), hbm),
        bias_grad=(jax.ShapeDtypeStruct((1, F), F32), vm),
    )
    scratch = dict(
        nf=b(N, F),
        tile_buf=b(NT, T, T),
        turned=b(NT, T, T),
        acc_tiles_t=b(NT + 1, T, T),
        adj_t=b(SB * T, N),
        hot=b(HALO, N),
        hot_t=b(N, HALO),
        out_halo=b(Y * C, ZC, F),
        st1=b(Y * C, ZC, F),
        st2=b(Z, YCC, F),
        halo_z=b(Z, YCC, F),
        hub=b(Y, ZQ, RES, C, HD, F),
        acc=f(F + 16, N),
        inv=f(8, N),
        selfc=b(R, D),
        meanc=b(R, D),
        ogc=b(R, D),
        wfull=b(2 * D, D),
        bias8=f(8, F),
        biasc=f(8, D),
        mean=b(N, F),
        pre=f(R, D),
        lo_send=b(R, D),
        lo_recv=b(X, R, F),
        wv=b(2 * D, F),
        ogv=b(N, F),
        wg_all=f(C * Y, DY, F),
        wb_all=b(C * Y, DY, F),
        gp=b(R, D),
        gm_send=b(X, R, F),
        gm=b(X, R, F),
        gs_send=b(X, R, F),
        gs_recv=b(X, R, F),
        wg32=f(C, D, D),
        wgb=b(C, D, D),
        wg_core=b(C, D, D),
        wx_send=b(X, D + 16, F),
        wx_recv=b(X, D + 16, F),
        wx_own=f(X, D + 8, F),
        wy_send=b(Y, DY + 16, F),
        wy_recv=b(Y, DY + 16, F),
        wy_own=f(Y, DY, F),
        wn_own=f(RES, DN, F),
        wn_send=b(RES, DN + 16, F),
        wn_recv=b(RES, DN + 16, F),
        wf_all=b(ZQ, DN + 16, F),
        wa=b(RES, DN, F),
        bias_core=f(C, 8, F),
        hs32=f(C, Y, Z, HD, F),
        hsb=b(C, Y, Z, HD, F),
        hs_core=b(Y, Z, HD, F),
        hy_send=b(Y, Z, HD, F),
        hy_recv=b(Y, Z, HD, F),
        hy_own=f(Z, HD, F),
        hz_own=f(RES, ZQ, HD, F),
        hz_send=b(RES, ZQ, HD, F),
        hz_recv=b(RES, ZQ, HD, F),
        hf_own=f(ZQ, HD, F),
        hf_send=b(ZQ, HD, F),
        hf_recv=b(ZQ, HD, F),
        halo_zb=b(Z, YCC, F),
        rt1=b(Z, YCC, F),
        halo_m=b(Y * C, ZC, F),
        rt2=b(Y * C, ZC, F),
        total=f(N, F),
        ng=b(N, F),
        local_sem=pltpu.SemaphoreType.DMA((8,)),
        s_yc=sem(Y * C),
        s_z=sem(Z),
        s_hz=sem(ZQ),
        s_hy=sem(Y),
        s_hc=sem(Y),
        s_xs=sem(X),
        s_xo=sem(X),
        s_xw=sem(X),
        s_xb=sem(X),
        s_wc=sem(X),
        s_xm=sem(X),
        s_xl=sem(X),
        s_xg=sem(X),
        s_xgs=sem(X),
        s_gc=sem(C),
        s_gx=sem(X),
        s_gy=sem(Y),
        s_gn=sem(RES),
        s_gf=sem(ZQ),
        s_az=sem(RES),
        s_ay=sem(Y * C),
        s_bc=sem(C),
        s_bhc=sem(Y),
        s_bhy=sem(Y),
        s_bhn=sem(RES),
        s_bhf=sem(ZQ),
        s_hn=sem(RES),
        s_rz=sem(Z),
        s_ryc=sem(Y * C),
    )
    names = list(inputs) + list(outputs) + list(scratch)
    results = pl.pallas_call(
        functools.partial(kernel, dims, names),
        out_shape=[shape for shape, _ in outputs.values()],
        in_specs=[spec for _, spec in inputs.values()],
        out_specs=[spec for _, spec in outputs.values()],
        scratch_shapes=list(scratch.values()),
        compiler_params=pltpu.CompilerParams(
            collective_id=0, has_side_effects=True, vmem_limit_bytes=60 * 1024 * 1024
        ),
    )(*[array for array, _ in inputs.values()])
    layer_out, node_grad, weight_grad, bias_grad = pl.pallas_call(
        copy_kernel,
        out_shape=[jax.ShapeDtypeStruct(v.shape, v.dtype) for v in results],
        in_specs=[vm] * 4,
        out_specs=[vm] * 4,
    )(*results)
    return (
        layer_out.reshape(N, F),
        node_grad,
        weight_grad.reshape(2 * D, F),
        bias_grad.reshape(F),
    )


def solution(mesh, y_chips=Y_CHIPS):
    dom, feat = mesh.shape["dom"], mesh.shape["feat"]
    sizes = (y_chips, dom // (CORES * y_chips), CORES, feat)
    in_specs = (
        P("dom", "feat"),
        P(None, "feat"),
        P("feat"),
        P("dom", "feat"),
        P("dom", None, None),
        P("dom"),
        P("dom"),
        P("dom"),
        P("dom"),
        P("dom", None),
    )
    out_specs = (P("dom", "feat"), P("dom", "feat"), P(None, "feat"), P("feat"))
    return jax.shard_map(
        functools.partial(per_device, sizes),
        mesh=mesh,
        in_specs=in_specs,
        out_specs=out_specs,
        check_vma=False,
    )
```

```python
import functools
import math
import types

import jax
import jax.numpy as jnp
from jax import lax
from jax.experimental import pallas as pl
from jax.experimental.pallas import tpu as pltpu
from jax.sharding import PartitionSpec as P

BF16 = jnp.bfloat16
F32 = jnp.float32
CORES = 2
Y_CHIPS = 4


def dot(a, b):
    return jnp.dot(a, b, preferred_element_type=F32)


def dot_nt(a, b):
    return lax.dot_general(a, b, (((1,), (1,)), ((), ())), preferred_element_type=F32)


def dot_tn(a, b):
    return lax.dot_general(a, b, (((0,), (0,)), ((), ())), preferred_element_type=F32)


class Group:
    def __init__(self, size, me, device):
        self.size, self.me, self.device = size, me, device

    def each(self, body):
        for step in range(1, self.size):
            body((self.me + step) & (self.size - 1))


class Exchange:
    def __init__(self, group, src, dst, sems, sent, landed, each=False):
        self.group, self.src, self.dst, self.sems = group, src, dst, sems
        self.sent, self.landed, self.one_by_one = sent, landed, each

    def copy(self, peer, landing):
        return pltpu.make_async_remote_copy(
            src_ref=self.src(peer),
            dst_ref=self.dst(landing),
            send_sem=self.sems.at[0, 0],
            recv_sem=self.sems.at[1, landing if self.one_by_one else 0],
            device_id=self.group.device(peer),
            device_id_type=pl.DeviceIdType.MESH,
        )

    def all(self, part):
        return pltpu.make_async_remote_copy(
            src_ref=part,
            dst_ref=part,
            send_sem=self.sems.at[0, 0],
            recv_sem=self.sems.at[1, 0],
            device_id=self.group.device((self.group.me + 1) & (self.group.size - 1)),
            device_id_type=pl.DeviceIdType.MESH,
        )

    def start_to(self, peer):
        self.copy(peer, self.group.me).start()

    def start(self):
        self.group.each(self.start_to)

    def wait(self):
        if self.group.size == 1:
            return
        self.all(self.landed).wait_recv()

    def wait_then(self, after):
        def body(peer):
            self.copy(peer, peer).wait_recv()
            after(peer)

        self.group.each(body)

    def drain(self):
        if self.group.size == 1:
            return
        self.all(self.sent).wait_send()


class Relay:
    def __init__(self, device, sems, src, dst):
        self.device, self.sems, self.src, self.dst = device, sems, src, dst

    def copy(self, slot):
        return pltpu.make_async_remote_copy(
            src_ref=self.src(slot),
            dst_ref=self.dst(slot),
            send_sem=self.sems.at[0, slot],
            recv_sem=self.sems.at[1, slot],
            device_id=self.device,
            device_id_type=pl.DeviceIdType.MESH,
        )

    def start(self, slot):
        self.copy(slot).start()


def log2(n):
    return n.bit_length() - 1


def div_(a, n):
    return lax.shift_right_logical(a, log2(n))


def mod_(a, n):
    return a & (n - 1)


def aligned(start, size):
    return pl.ds(pl.multiple_of(start, size), size)


def kernel(dims, names, *refs):
    r = types.SimpleNamespace(**dict(zip(names, refs)))
    Y, Z, C, X, N, T, NT, F, HD, CUT, scale = dims
    D = X * F
    R = N // X
    DOM = Y * Z * C
    HALO = DOM * CUT
    NB = N // T
    SB = (N + HALO + DOM * HD) // T
    ZC, YCC = Z * CUT, Y * C * CUT
    PERY = Z * C * HD
    DY = D // Y
    RES = Z // 4 if Z >= 8 else Z
    ZQ = Z // RES
    DN = DY // RES
    dom, x = lax.axis_index("dom"), lax.axis_index("feat")
    c = dom & (C - 1)
    z = (dom >> log2(C)) & (Z - 1)
    y = dom >> log2(C * Z)
    yc = y * C + c

    def at(yy, zz, cc):
        return ((yy * Z + zz) * C + cc, x)

    gyc = Group(Y * C, yc, lambda p: at(p >> log2(C), z, p & (C - 1)))
    gz = Group(Z, z, lambda p: at(y, p, c))
    gy = Group(Y, y, lambda p: at(p, z, c))
    zr, zq = z & (RES - 1), z >> log2(RES)

    def near(p):
        step = (p - zr) & (RES - 1)
        step = jnp.where(step > RES // 2, step - RES, step)
        return at(y, (z + step) & (Z - 1), c)

    gfar = Group(Z // RES, zq, lambda p: at(y, (p << log2(RES)) | zr, c))
    gnear = Group(RES, zr, near)
    gc = Group(C, c, lambda p: at(y, z, p))
    gx = Group(X, x, lambda p: (dom, p))
    other_core = at(y, z, 1 - c)

    barrier = pltpu.get_barrier_semaphore()
    for group in (gyc, gz, gx):
        group.each(
            lambda peer, group=group: pl.semaphore_signal(
                barrier, inc=1, device_id=group.device(peer), device_id_type=pl.DeviceIdType.MESH
            )
        )

    def rows_of(p):
        return aligned(p * R, R)

    def cols_of(p):
        return aligned(p * F, F)

    def local(i, src, dst):
        return pltpu.make_async_copy(src, dst, r.local_sem.at[i])

    fetch_nf = local(0, r.node_feats, r.nf)
    fetch_tiles = local(1, r.tiles, r.tile_buf)
    fetch_w = local(2, r.weight, r.wv)
    fetch_og = local(3, r.out_grad, r.ogv)
    fetch_nf.start()
    fetch_w.start()
    fetch_og.start()
    fetch_tiles.start()

    eye = lax.broadcasted_iota(jnp.int32, (DOM, DOM), 0) == lax.broadcasted_iota(
        jnp.int32, (DOM, DOM), 1
    )
    for k in range(CUT):
        wide = jnp.broadcast_to(r.sends[k : k + 1, :], (DOM, DOM)).astype(F32)
        col = jnp.sum(jnp.where(eye, wide, 0.0), axis=1, keepdims=True).astype(jnp.int32)
        r.hot[k * DOM : (k + 1) * DOM, :] = (
            col == lax.broadcasted_iota(jnp.int32, (DOM, N), 1)
        ).astype(BF16)
    eye = lax.broadcasted_iota(jnp.int32, (HD, HD), 0) == lax.broadcasted_iota(
        jnp.int32, (HD, HD), 1
    )
    wide = jnp.broadcast_to(r.hub_ids[...], (HD, HD)).astype(F32)
    col = jnp.sum(jnp.where(eye, wide, 0.0), axis=1, keepdims=True).astype(jnp.int32)
    hub_hot = (col == lax.broadcasted_iota(jnp.int32, (HD, N), 1)).astype(BF16)

    def perm(source_of):
        row = lax.broadcasted_iota(jnp.int32, (HALO, HALO), 0)
        lane = lax.broadcasted_iota(jnp.int32, (HALO, HALO), 1)
        return (source_of(row) == lane).astype(BF16)

    def peer_major(i):
        k, zz = mod_(i, CUT), mod_(div_(i, CUT), Z)
        cc, yy = mod_(div_(i, ZC), C), div_(i, ZC * C)
        return k * DOM + (yy * Z + zz) * C + cc

    def z_major(i):
        return (mod_(div_(i, CUT), Y * C) * Z + div_(i, YCC)) * CUT + mod_(i, CUT)

    def yc_major(i):
        return (mod_(div_(i, CUT), Z) * (Y * C) + div_(i, ZC)) * CUT + mod_(i, CUT)

    def to_dom(i):
        yy = div_(i, Z * C * CUT)
        zz = mod_(div_(i, C * CUT), Z)
        return (zz * Y + yy) * (C * CUT) + mod_(i, C * CUT)

    def from_dom(i):
        zz = div_(i, Y * C * CUT)
        yy = mod_(div_(i, C * CUT), Y)
        return (yy * Z + zz) * (C * CUT) + mod_(i, C * CUT)

    fetch_nf.wait()
    r.hub[y, zq, zr, c] = dot(hub_hot, r.nf[...]).astype(BF16)
    picked = dot(r.hot[...], r.nf[...]).astype(BF16)
    r.out_halo[...] = dot(perm(peer_major), picked).astype(BF16).reshape(Y * C, ZC, F)
    r.bias8[...] = jnp.broadcast_to(r.bias[...], (8, F))
    pl.semaphore_wait(barrier, Y * C + Z + X - 3)

    done = []

    def most(ref):
        return ref.at[pl.ds(0, ref.shape[0] - 1)]

    def cols3(ref):
        return ref.at[:, 0 : D - F]


    def exchange(group, src, dst, sems, sent, landed, each=False):
        ex = Exchange(group, src, dst, sems, sent, landed, each)
        done.append(ex)
        return ex

    ex_yc = exchange(
        gyc, lambda p: r.out_halo.at[p], lambda p: r.st1.at[p],
        r.s_yc,
        most(r.out_halo),
        most(r.st1),
    )
    ex_yc.start()
    ex_hz = exchange(
        gfar,
        lambda p: r.hub.at[y, zq, zr, c],
        lambda p: r.hub.at[y, p, zr, c],
        r.s_hz,
        r.hub.at[y, pl.ds(0, ZQ - 1), zr, c],
        r.hub.at[y, pl.ds(0, ZQ - 1), zr, c],
    )
    ex_hz.start()
    r.st1[yc] = r.out_halo[yc]

    wrows = aligned(c * D, D)
    fetch_w.wait()
    fetch_og.wait()
    ex_xw = exchange(
        gx, lambda p: r.wv.at[wrows], lambda p: r.wfull.at[wrows, cols_of(p)],
        r.s_xw,
        r.wfull.at[wrows, 0 : D - F],
        r.wfull.at[wrows, 0 : D - F],
        each=True,
    )
    ex_xw.start()
    ex_xs = exchange(
        gx, lambda p: r.nf.at[rows_of(p)], lambda p: r.selfc.at[:, cols_of(p)],
        r.s_xs,
        cols3(r.selfc),
        cols3(r.selfc),
    )
    ex_xs.start()
    ex_xb = exchange(
        gx, lambda p: r.bias8, lambda p: r.biasc.at[:, cols_of(p)],
        r.s_xb,
        cols3(r.biasc),
        cols3(r.biasc),
    )
    ex_xb.start()
    ex_xo = exchange(
        gx, lambda p: r.ogv.at[rows_of(p)], lambda p: r.ogc.at[:, cols_of(p)],
        r.s_xo,
        cols3(r.ogc),
        cols3(r.ogc),
    )
    ex_xo.start()
    r.biasc[:, cols_of(x)] = r.bias8[...]
    r.selfc[:, cols_of(x)] = r.nf[rows_of(x), :]
    r.ogc[:, cols_of(x)] = r.ogv[rows_of(x), :]
    r.wfull[:, cols_of(x)] = r.wv[...]

    fetch_tiles.wait()
    turn = NT // 8 if NT % 8 == 0 else 1

    def turn_tiles(i, carry):
        for k in range(NT // turn):
            t = i * (NT // turn) + k
            r.turned[t] = r.tile_buf[t].T
        return carry

    lax.fori_loop(0, turn, turn_tiles, 0)
    r.acc_tiles_t[0] = jnp.zeros((T, T), BF16)

    ex_hz.wait()
    ex_hn = exchange(
        gnear,
        lambda p: r.hub.at[y, :, zr, c],
        lambda p: r.hub.at[y, :, p, c],
        r.s_hn,
        r.hub.at[y, :, pl.ds(0, RES - 1), c],
        r.hub.at[y, :, pl.ds(0, RES - 1), c],
    )
    ex_hn.start()

    def add_tile(t, carry):
        r.acc_tiles_t[t + 1] = r.turned[t] + r.acc_tiles_t[r.prev[t]]
        return carry

    lax.fori_loop(0, NT, add_tile, 0)

    ex_yc.wait()
    r.halo_z[...] = (
        dot(perm(z_major), r.st1[...].reshape(HALO, F)).astype(BF16).reshape(Z, YCC, F)
    )
    ex_z = exchange(
        gz, lambda p: r.halo_z.at[p], lambda p: r.st2.at[p],
        r.s_z,
        most(r.halo_z),
        most(r.st2),
    )
    ex_z.start()
    r.st2[z] = r.halo_z[z]

    ex_hn.wait()
    ex_hy = exchange(
        gy, lambda p: r.hub.at[y, :, :, c], lambda p: r.hub.at[p, :, :, c],
        r.s_hy,
        r.hub.at[pl.ds(0, Y - 1), :, :, c],
        r.hub.at[pl.ds(0, Y - 1), :, :, c],
        each=True,
    )
    ex_hy.start()
    hub_to = Relay(other_core, r.s_hc, lambda p: r.hub.at[p, :, :, c], lambda p: r.hub.at[p, :, :, c])
    hub_from = Relay(
        other_core, r.s_hc, lambda p: r.hub.at[p, :, :, 1 - c], lambda p: r.hub.at[p, :, :, 1 - c]
    )
    hub_to.start(y)

    w_to = Relay(
        other_core,
        r.s_wc,
        lambda p: r.wfull.at[wrows, cols_of(p)],
        lambda p: r.wfull.at[wrows, cols_of(p)],
    )
    other_rows = aligned((1 - c) * D, D)
    w_from = Relay(
        other_core,
        r.s_wc,
        lambda p: r.wfull.at[other_rows, cols_of(p)],
        lambda p: r.wfull.at[other_rows, cols_of(p)],
    )
    def place(s, carry):
        for n in range(NB):
            r.adj_t[aligned(s * T, T), n * T : (n + 1) * T] = r.acc_tiles_t[r.last[n * SB + s]]
        return carry

    lax.fori_loop(0, SB, place, 0)

    def gather(rows, source):
        ones = jnp.ones((16, source.shape[0]), BF16)
        return dot(jnp.concatenate([source.T, ones], axis=0), r.adj_t[rows, :])

    def add_hub(p):
        rows = pl.ds(pl.multiple_of(N + HALO + p * PERY, T), PERY)
        r.acc[...] += gather(rows, r.hub[p].reshape(PERY, F))

    r.acc[...] = gather(slice(0, N), r.nf[...])
    hub_from.copy(y).wait_recv()
    add_hub(y)

    ex_xw.wait_then(w_to.start)
    ex_hy.wait_then(hub_to.start)

    ex_z.wait()
    halo = dot(perm(to_dom), r.st2[...].reshape(HALO, F)).astype(BF16)
    r.acc[...] += gather(slice(N, N + HALO), halo)

    for i in range(1, Y):
        p = (y + i) & (Y - 1)
        hub_from.copy(p).wait_recv()
        add_hub(p)
    r.inv[...] = 1.0 / jnp.maximum(r.acc[F : F + 8, :], 1.0)
    r.mean[...] = (r.acc[0:F, :] * r.inv[0:1, :]).astype(BF16).T
    ex_xm = exchange(
        gx, lambda p: r.mean.at[rows_of(p)], lambda p: r.meanc.at[:, cols_of(p)],
        r.s_xm,
        cols3(r.meanc),
        cols3(r.meanc),
    )
    ex_xm.start()
    r.meanc[:, cols_of(x)] = r.mean[rows_of(x), :]

    ex_xs.wait()
    ex_xb.wait()
    ex_xo.wait()
    gx.each(lambda peer: w_from.copy(peer).wait_recv())
    r.pre[...] = dot(r.selfc[...], r.wfull[0:D, :]) + r.biasc[0:1, :]

    for k in range(CUT):
        row = jnp.broadcast_to(r.sends[k : k + 1, :], (N, DOM))
        r.hot_t[:, k * DOM : (k + 1) * DOM] = (
            row == lax.broadcasted_iota(jnp.int32, (N, DOM), 0)
        ).astype(BF16)

    inv_rows = jnp.broadcast_to(r.inv[0:1, rows_of(x)], (F, R)).T
    ex_xm.wait()
    pre_act = r.pre[...] + dot(r.meanc[...], r.wfull[D : 2 * D, :])
    sig = jax.nn.sigmoid(pre_act)
    r.gp[...] = (r.ogc[...].astype(F32) * (sig * (1.0 + pre_act * (1.0 - sig)))).astype(BF16)
    r.lo_send[...] = (pre_act * sig).astype(BF16)
    cat_mean = dot_nt(r.gp[...], r.wfull[D : 2 * D, :])
    for j in range(X):
        r.gm_send[j] = (cat_mean[:, j * F : (j + 1) * F] * inv_rows).astype(BF16)
    ex_xg = exchange(
        gx, lambda p: r.gm_send.at[p], lambda p: r.gm.at[p],
        r.s_xg,
        most(r.gm_send),
        most(r.gm),
    )
    ex_xg.start()
    r.gm[x] = r.gm_send[x]

    for half, src in enumerate((r.selfc, r.meanc)):
        for q in range(0, D, 2 * T):
            part = dot_tn(src[:, q : q + 2 * T], r.gp[...])
            r.wg32[half, q : q + 2 * T, :] = part
            r.wgb[half, q : q + 2 * T, :] = part.astype(BF16)
    ex_gc = exchange(
        gc, lambda p: r.wgb.at[p], lambda p: r.wg_core.at[p],
        r.s_gc,
        most(r.wgb),
        most(r.wg_core),
    )
    ex_gc.start()
    bias_sum = jnp.sum(r.gp[...].astype(F32), axis=0, keepdims=True)

    def bias_rows(value):
        full = jnp.broadcast_to(value, (8, F))
        high = full.astype(BF16).astype(F32)
        return jnp.concatenate([high, full - high], axis=0).astype(BF16)

    def bias_of(rows):
        wide = rows.astype(F32)
        return wide[0:8] + wide[8:16]

    ex_xg.wait()
    core_to = Relay(
        other_core, r.s_bhc, lambda p: r.hsb.at[1 - c, p], lambda p: r.hs_core.at[p]
    )
    ex_bhy = exchange(
        gy, lambda p: r.hy_send.at[p], lambda p: r.hy_recv.at[p],
        r.s_bhy,
        most(r.hy_send),
        most(r.hy_recv),
    )

    def spread(rows):
        return dot(r.adj_t[rows, :], r.gm[...].reshape(N, F))

    def back_hub(p):
        rows = spread(pl.ds(pl.multiple_of(N + HALO + p * PERY, T), PERY)).reshape(Z, C, HD, F)
        for cc in range(C):
            r.hs32[cc, p] = rows[:, cc]
            r.hsb[cc, p] = rows[:, cc].astype(BF16)
        core_to.start(p)

    def pair_hub(p, own):
        core_to.copy(p).wait_recv()
        pair = r.hs32[c, p] + r.hs_core[p].astype(F32)
        if own:
            r.hy_own[...] = pair
        else:
            r.hy_send[p] = pair.astype(BF16)
            ex_bhy.start_to(p)

    order = [(y + i) & (Y - 1) for i in range(1, Y)] + [y]
    back_hub(order[0])

    ex_gc.wait()
    for j in range(X):
        cols = slice(j * F, (j + 1) * F)
        block = r.wg32[c, :, cols] + r.wg_core[1 - c, :, cols].astype(F32)
        r.wx_own[j, 0:D, :] = block
        r.wx_send[j, 0:D, :] = block.astype(BF16)
        r.wx_own[j, D : D + 8, :] = jnp.broadcast_to(bias_sum[:, cols], (8, F))
        r.wx_send[j, D : D + 16, :] = bias_rows(bias_sum[:, cols])
    ex_gx = exchange(
        gx, lambda p: r.wx_send.at[p], lambda p: r.wx_recv.at[p],
        r.s_gx,
        most(r.wx_send),
        most(r.wx_recv),
    )
    ex_gx.start()

    for i in range(1, Y):
        back_hub(order[i])
        pair_hub(order[i - 1], False)

    halo_b = spread(slice(N, N + HALO)).astype(BF16)
    r.halo_zb[...] = dot(perm(from_dom), halo_b).astype(BF16).reshape(Z, YCC, F)
    ex_rz = exchange(
        gz, lambda p: r.halo_zb.at[p], lambda p: r.rt1.at[p],
        r.s_rz,
        most(r.halo_zb),
        most(r.rt1),
    )
    ex_rz.start()
    r.rt1[z] = r.halo_zb[z]

    pair_hub(y, True)

    r.wx_recv[x] = jnp.zeros((D + 16, F), BF16)
    ex_gx.wait()
    wsum = r.wx_own[x, 0:D, :]
    bsum = r.wx_own[x, D : D + 8, :]
    for j in range(X):
        wsum = wsum + r.wx_recv[j, 0:D, :].astype(F32)
        bsum = bsum + bias_of(r.wx_recv[j, D : D + 16, :])
    for j in range(Y):
        block = wsum[j * DY : (j + 1) * DY]
        r.wy_own[j] = block
        r.wy_send[j, 0:DY, :] = block.astype(BF16)
        r.wy_send[j, DY : DY + 16, :] = bias_rows(bsum[0:1])
    ex_gy = exchange(
        gy, lambda p: r.wy_send.at[p], lambda p: r.wy_recv.at[p],
        r.s_gy,
        most(r.wy_send),
        most(r.wy_recv),
    )
    ex_gy.start()

    cat_self = dot_nt(r.gp[...], r.wfull[0:D, :])
    for j in range(X):
        r.gs_send[j] = cat_self[:, j * F : (j + 1) * F].astype(BF16)
    ex_xgs = exchange(
        gx, lambda p: r.gs_send.at[p], lambda p: r.gs_recv.at[p],
        r.s_xgs,
        most(r.gs_send),
        most(r.gs_recv),
    )
    ex_xgs.start()
    ex_xl = exchange(
        gx, lambda p: r.lo_send.at[:, cols_of(p)], lambda p: r.lo_recv.at[p],
        r.s_xl,
        cols3(r.lo_send),
        most(r.lo_recv),
    )
    ex_xl.start()
    r.lo_recv[x] = r.lo_send[:, cols_of(x)]
    r.gs_recv[x] = r.gs_send[x]

    r.wy_recv[y] = jnp.zeros((DY + 16, F), BF16)
    ex_gy.wait()
    wsum = r.wy_own[y]
    for j in range(Y):
        wsum = wsum + r.wy_recv[j, 0:DY, :].astype(F32)
        bsum = bsum + bias_of(r.wy_recv[j, DY : DY + 16, :])
    for p in range(RES):
        block = wsum[p * DN : (p + 1) * DN]
        r.wn_own[p] = block
        r.wn_send[p, 0:DN, :] = block.astype(BF16)
        r.wn_send[p, DN : DN + 16, :] = bias_rows(bsum[0:1])
    ex_gn = exchange(
        gnear,
        lambda p: r.wn_send.at[p],
        lambda p: r.wn_recv.at[p],
        r.s_gn,
        most(r.wn_send),
        most(r.wn_recv),
    )
    ex_gn.start()

    r.total[...] = spread(slice(0, N))

    r.wn_recv[zr] = jnp.zeros((DN + 16, F), BF16)
    ex_gn.wait()
    wsum = r.wn_own[zr]
    for p in range(RES):
        wsum = wsum + r.wn_recv[p, 0:DN, :].astype(F32)
        bsum = bsum + bias_of(r.wn_recv[p, DN : DN + 16, :])
    r.wf_all[zq, 0:DN, :] = wsum.astype(BF16)
    r.wf_all[zq, DN : DN + 16, :] = bias_rows(bsum[0:1])
    ex_gf = exchange(
        gfar,
        lambda p: r.wf_all.at[zq],
        lambda p: r.wf_all.at[p],
        r.s_gf,
        most(r.wf_all),
        most(r.wf_all),
    )
    ex_gf.start()

    r.hy_recv[y] = jnp.zeros((Z, HD, F), BF16)
    ex_bhy.wait()
    hub_y = r.hy_own[...]
    for p in range(Y):
        hub_y = hub_y + r.hy_recv[p].astype(F32)
    hub_y = hub_y.reshape(ZQ, RES, HD, F)
    for p in range(RES):
        r.hz_own[p] = hub_y[:, p]
        r.hz_send[p] = hub_y[:, p].astype(BF16)
    ex_bhn = exchange(
        gnear,
        lambda p: r.hz_send.at[p],
        lambda p: r.hz_recv.at[p],
        r.s_bhn,
        most(r.hz_send),
        most(r.hz_recv),
    )
    ex_bhn.start()

    ex_rz.wait()
    r.halo_m[...] = (
        dot(perm(yc_major), r.rt1[...].reshape(HALO, F)).astype(BF16).reshape(Y * C, ZC, F)
    )
    ex_ryc = exchange(
        gyc, lambda p: r.halo_m.at[p], lambda p: r.rt2.at[p],
        r.s_ryc,
        most(r.halo_m),
        most(r.rt2),
    )
    ex_ryc.start()
    r.rt2[yc] = r.halo_m[yc]

    r.hz_recv[zr] = jnp.zeros((ZQ, HD, F), BF16)
    ex_bhn.wait()
    hub_z = r.hz_own[zr] + jnp.sum(r.hz_recv[...].astype(F32), axis=0)
    r.hf_own[...] = hub_z
    r.hf_send[...] = hub_z.astype(BF16)
    ex_bhf = exchange(
        gfar,
        lambda p: r.hf_send.at[p],
        lambda p: r.hf_recv.at[p],
        r.s_bhf,
        most(r.hf_send),
        most(r.hf_recv),
    )
    ex_bhf.start()

    ex_gf.wait()
    for q in range(ZQ):
        far = r.wf_all[q].astype(F32)
        wtotal = far[0:DN] if q == 0 else wtotal + far[0:DN]
        btotal = bias_of(far[DN : DN + 16]) + (0.0 if q == 0 else btotal)
    r.wa[zr] = (wtotal * scale).astype(BF16)
    r.bias_core[c] = btotal * scale
    ex_az = exchange(
        gnear, lambda p: r.wa.at[zr], lambda p: r.wa.at[p], r.s_az, most(r.wa), most(r.wa)
    )
    ex_az.start()
    ex_bc = exchange(
        gc, lambda p: r.bias_core.at[c], lambda p: r.bias_core.at[p],
        r.s_bc,
        most(r.bias_core),
        most(r.bias_core),
    )
    ex_bc.start()

    ex_xgs.wait()
    for j in range(X):
        r.total[j * R : (j + 1) * R, :] += r.gs_recv[j].astype(F32)

    ex_ryc.wait()
    returned = dot(perm(from_peer_major(dims)), r.rt2[...].reshape(HALO, F)).astype(BF16)
    r.total[...] += dot(r.hot_t[...], returned)

    ex_az.wait()
    r.wb_all[yc_row(c, Y, y)] = r.wa[...].reshape(DY, F)
    ex_ay = exchange(
        gyc,
        lambda p: r.wb_all.at[yc_row(c, Y, y)],
        lambda p: r.wb_all.at[yc_row(p & (C - 1), Y, p >> log2(C))],
        r.s_ay,
        most(r.wb_all),
        most(r.wb_all),
    )
    ex_ay.start()

    r.hf_recv[zq] = jnp.zeros((HD, F), BF16)
    ex_bhf.wait()
    hub_mine = r.hf_own[zq] + jnp.sum(r.hf_recv[...].astype(F32), axis=0)
    high = hub_mine.astype(BF16)
    low = (hub_mine - high.astype(F32)).astype(BF16)
    hub_hot_t = (
        jnp.broadcast_to(r.hub_ids[...], (N, HD)) == lax.broadcasted_iota(jnp.int32, (N, HD), 0)
    ).astype(BF16)
    r.ng[...] = (r.total[...] + dot(hub_hot_t, high) + dot(hub_hot_t, low)).astype(BF16)
    ng_out = local(6, r.ng, r.node_grad)
    ng_out.start()


    ex_xl.wait()
    lo_out = local(5, r.lo_recv, r.layer_out)
    lo_out.start()

    ex_bc.wait()
    r.bias_grad[...] = r.bias_core[0, 0:1] + r.bias_core[1, 0:1]
    ex_ay.wait()
    r.wg_all[...] = r.wb_all[...].astype(F32)

    w_out = local(7, r.wg_all, r.weight_grad)
    w_out.start()
    lo_out.wait()
    ng_out.wait()
    w_out.wait()
    for ex in done:
        ex.drain()
    for p in range(Y):
        hub_to.copy(p).wait_send()
        core_to.copy(p).wait_send()
    gx.each(lambda peer: w_to.copy(peer).wait_send())


def yc_row(c, Y, y):
    return c * Y + y


def from_peer_major(dims):
    Y, Z, C, CUT = dims[0], dims[1], dims[2], dims[9]
    DOM = Y * Z * C

    def source(i):
        k, q = div_(i, DOM), mod_(i, DOM)
        cc, zz, yy = mod_(q, C), mod_(div_(q, C), Z), div_(q, C * Z)
        return ((yy * C + cc) * Z + zz) * CUT + k

    return source


def copy_kernel(*refs):
    n = len(refs) // 2
    for src, dst in zip(refs[:n], refs[n:]):
        dst[...] = src[...]


def per_device(
    sizes,
    node_feats,
    neigh_weight,
    bias,
    out_grad,
    tile_values,
    tile_src,
    tile_dst,
    tile_count,
    hub_rows,
    send_rows,
):
    Y, Z, C, X = sizes
    N, F = node_feats.shape
    NT, T = tile_values.shape[:2]
    CUT = send_rows.shape[1]
    HD = hub_rows.shape[0]
    DOM = Y * Z * C
    HALO = DOM * CUT
    NB, SB = N // T, (N + HALO + DOM * HD) // T
    D, R = X * F, N // X
    ZC, YCC = Z * CUT, Y * C * CUT
    DY = D // Y
    RES = Z // 4 if Z >= 8 else Z
    ZQ = Z // RES
    DN = DY // RES

    at = jnp.arange(NT, dtype=jnp.int32)
    key = jnp.where(at < tile_count[0], tile_dst * SB + tile_src, -1)
    same = (key[:, None] == key[None, :]) & (at[None, :] < at[:, None])
    prev = jnp.max(jnp.where(same, at[None, :] + 1, 0), axis=1)
    place = jnp.arange(NB * SB, dtype=jnp.int32)
    last = jnp.max(jnp.where(place[:, None] == key[None, :], at[None, :] + 1, 0), axis=1)

    dims = (Y, Z, C, X, N, T, NT, F, HD, CUT, 1.0 / math.sqrt(N * DOM))
    vm = pl.BlockSpec(memory_space=pltpu.VMEM)
    sm = pl.BlockSpec(memory_space=pltpu.SMEM)
    hbm = pl.BlockSpec(memory_space=pl.ANY)

    def b(*shape):
        return pltpu.VMEM(shape, BF16)

    def f(*shape):
        return pltpu.VMEM(shape, F32)

    def sem(n):
        return pltpu.SemaphoreType.DMA((2, n))

    inputs = dict(
        node_feats=(node_feats, hbm),
        weight=(neigh_weight, hbm),
        out_grad=(out_grad, hbm),
        tiles=(tile_values, hbm),
        bias=(bias[None, :], vm),
        sends=(send_rows.T, vm),
        hub_ids=(hub_rows[None, :], vm),
        prev=(prev, sm),
        last=(last, sm),
    )
    outputs = dict(
        layer_out=(jax.ShapeDtypeStruct((X, R, F), BF16), hbm),
        node_grad=(jax.ShapeDtypeStruct((N, F), BF16), hbm),
        weight_grad=(jax.ShapeDtypeStruct((C * Y, DY, F), F32), hbm),
        bias_grad=(jax.ShapeDtypeStruct((1, F), F32), vm),
    )
    scratch = dict(
        nf=b(N, F),
        tile_buf=b(NT, T, T),
        turned=b(NT, T, T),
        acc_tiles_t=b(NT + 1, T, T),
        adj_t=b(SB * T, N),
        hot=b(HALO, N),
        hot_t=b(N, HALO),
        out_halo=b(Y * C, ZC, F),
        st1=b(Y * C, ZC, F),
        st2=b(Z, YCC, F),
        halo_z=b(Z, YCC, F),
        hub=b(Y, ZQ, RES, C, HD, F),
        acc=f(F + 16, N),
        inv=f(8, N),
        selfc=b(R, D),
        meanc=b(R, D),
        ogc=b(R, D),
        wfull=b(2 * D, D),
        bias8=f(8, F),
        biasc=f(8, D),
        mean=b(N, F),
        pre=f(R, D),
        lo_send=b(R, D),
        lo_recv=b(X, R, F),
        wv=b(2 * D, F),
        ogv=b(N, F),
        wg_all=f(C * Y, DY, F),
        wb_all=b(C * Y, DY, F),
        gp=b(R, D),
        gm_send=b(X, R, F),
        gm=b(X, R, F),
        gs_send=b(X, R, F),
        gs_recv=b(X, R, F),
        wg32=f(C, D, D),
        wgb=b(C, D, D),
        wg_core=b(C, D, D),
        wx_send=b(X, D + 16, F),
        wx_recv=b(X, D + 16, F),
        wx_own=f(X, D + 8, F),
        wy_send=b(Y, DY + 16, F),
        wy_recv=b(Y, DY + 16, F),
        wy_own=f(Y, DY, F),
        wn_own=f(RES, DN, F),
        wn_send=b(RES, DN + 16, F),
        wn_recv=b(RES, DN + 16, F),
        wf_all=b(ZQ, DN + 16, F),
        wa=b(RES, DN, F),
        bias_core=f(C, 8, F),
        hs32=f(C, Y, Z, HD, F),
        hsb=b(C, Y, Z, HD, F),
        hs_core=b(Y, Z, HD, F),
        hy_send=b(Y, Z, HD, F),
        hy_recv=b(Y, Z, HD, F),
        hy_own=f(Z, HD, F),
        hz_own=f(RES, ZQ, HD, F),
        hz_send=b(RES, ZQ, HD, F),
        hz_recv=b(RES, ZQ, HD, F),
        hf_own=f(ZQ, HD, F),
        hf_send=b(ZQ, HD, F),
        hf_recv=b(ZQ, HD, F),
        halo_zb=b(Z, YCC, F),
        rt1=b(Z, YCC, F),
        halo_m=b(Y * C, ZC, F),
        rt2=b(Y * C, ZC, F),
        total=f(N, F),
        ng=b(N, F),
        local_sem=pltpu.SemaphoreType.DMA((8,)),
        s_yc=sem(Y * C),
        s_z=sem(Z),
        s_hz=sem(ZQ),
        s_hy=sem(Y),
        s_hc=sem(Y),
        s_xs=sem(X),
        s_xo=sem(X),
        s_xw=sem(X),
        s_xb=sem(X),
        s_wc=sem(X),
        s_xm=sem(X),
        s_xl=sem(X),
        s_xg=sem(X),
        s_xgs=sem(X),
        s_gc=sem(C),
        s_gx=sem(X),
        s_gy=sem(Y),
        s_gn=sem(RES),
        s_gf=sem(ZQ),
        s_az=sem(RES),
        s_ay=sem(Y * C),
        s_bc=sem(C),
        s_bhc=sem(Y),
        s_bhy=sem(Y),
        s_bhn=sem(RES),
        s_bhf=sem(ZQ),
        s_hn=sem(RES),
        s_rz=sem(Z),
        s_ryc=sem(Y * C),
    )
    names = list(inputs) + list(outputs) + list(scratch)
    results = pl.pallas_call(
        functools.partial(kernel, dims, names),
        out_shape=[shape for shape, _ in outputs.values()],
        in_specs=[spec for _, spec in inputs.values()],
        out_specs=[spec for _, spec in outputs.values()],
        scratch_shapes=list(scratch.values()),
        compiler_params=pltpu.CompilerParams(
            collective_id=0, has_side_effects=True, vmem_limit_bytes=60 * 1024 * 1024
        ),
    )(*[array for array, _ in inputs.values()])
    layer_out, node_grad, weight_grad, bias_grad = pl.pallas_call(
        copy_kernel,
        out_shape=[jax.ShapeDtypeStruct(v.shape, v.dtype) for v in results],
        in_specs=[vm] * 4,
        out_specs=[vm] * 4,
    )(*results)
    return (
        layer_out.reshape(N, F),
        node_grad,
        weight_grad.reshape(2 * D, F),
        bias_grad.reshape(F),
    )


def solution(mesh, y_chips=Y_CHIPS):
    dom, feat = mesh.shape["dom"], mesh.shape["feat"]
    sizes = (y_chips, dom // (CORES * y_chips), CORES, feat)
    in_specs = (
        P("dom", "feat"),
        P(None, "feat"),
        P("feat"),
        P("dom", "feat"),
        P("dom", None, None),
        P("dom"),
        P("dom"),
        P("dom"),
        P("dom"),
        P("dom", None),
    )
    out_specs = (P("dom", "feat"), P("dom", "feat"), P(None, "feat"), P("feat"))
    return jax.shard_map(
        functools.partial(per_device, sizes),
        mesh=mesh,
        in_specs=in_specs,
        out_specs=out_specs,
        check_vma=False,
    )
```
